256 devices in a mesh: dp: 16 (over y, z_hi), mp: 16 (over z_lo, x, core).
Axes of the slice: x: 4, y: 4, z: 8 (z_hi: 4, z_lo: 2; z = z_hi * 2 + z_lo), core: 2. Of those that a mesh axis runs over, the one named last changes fastest.
Arguments:
- states: bfloat16 [32768, 4096], P(('dp', 'mp')), may hold values from -32 to 32
- positions: int32 [768], P(('dp', 'mp')), may hold values from 0 to 127, as said below
- counts: int32 [256], P(('dp', 'mp')), may hold values from 1 to 3, 384 in all
- targets: int32 [768], P(('dp', 'mp')), may hold values from 0 to 126975
- table: bfloat16 [126976, 4096], P(('dp', 'mp')), may hold values from -3 to 3
- h_pre: bfloat16 [768, 16384], P(None, 'mp'), may hold values from -6 to 6
- w_down: bfloat16 [16384, 4096], P('mp', 'dp'), may hold values from -0.375 to 0.375
Outputs:
- table_grad: bfloat16 [126976, 4096], P(('dp', 'mp'))
- w_down_grad: float32 [16384, 4096], P('mp', 'dp')
- hidden_grad: float32 [768, 16384], P('dp', 'mp')
The draws below stay inside these ranges and needn't reach their ends.
Inputs may be any that keep to these rules, and one draw needn't show every extreme that they name: `positions`: the 3 slots of each device name distinct tokens of that device's 128. Slot c of a device is live when c is below that device's count; the counts sum to 384.
All inputs are finite; a program needn't handle non-finite values.
Results may differ from the reference program's by a relative error of at most 0.005.
Values may be sent and summed in bfloat16 or wider, within the bound.
No kernel may reach another device: no remote copies, remote signals or barrier semaphores. Data moves between devices by JAX's collectives and lax.ppermute only.
A program may use at most 128 MiB of HBM per device.

```python
import math
import jax
import jax.numpy as jnp
import numpy as np
from jax import lax

D = 4096
FF = 16384
VOCAB = 126976
TOK_DEV = 128
CAP = 3
SLOTS = 768
TOTAL = 384
TOKENS = 32768
DEVICES = 256


def row_normals(key, indices):
    return jax.vmap(lambda index: jax.random.normal(jax.random.fold_in(key, index), (D,), jnp.float32))(indices)


def draw_table(key, part):
    base = row_normals(key, jnp.arange(VOCAB, dtype=jnp.int32))
    scale = 3.0 / math.sqrt(D)
    return (jnp.clip(base, -6.0, 6.0) * scale).astype(jnp.bfloat16)


def draw_states(key, part):
    key = jax.random.fold_in(key, 7)
    keys = jax.random.split(key, 1)
    values = jnp.clip(jax.random.normal(keys[0], (TOKENS, D), jnp.float32), -6.0, 6.0)
    return values.astype(jnp.bfloat16)


def draw_positions(key, part):
    key = jax.random.fold_in(key, 11)
    owners = SLOTS // CAP
    scores = jax.random.randint(key, (owners, TOK_DEV), 0, 1 << 20) * TOK_DEV + jnp.arange(TOK_DEV, dtype=jnp.int32)[None, :]
    order = jnp.argsort(scores, axis=1)[:, :CAP]
    return order.reshape(SLOTS).astype(jnp.int32)


def set_ends(result, key, low, high):
    shape = result.shape
    place = [jax.random.randint(jax.random.fold_in(key, axis), (), 0, shape[axis]) for axis in range(len(shape))]
    result = result.at[tuple(place)].set(low)
    longest = shape.index(max(shape))
    place[longest] = (place[longest] + 1) % shape[longest]
    return result.at[tuple(place)].set(high)


def levels(rng, dims, cuts, smallest, high):
    loudness, own = 1.0, jax.random.fold_in(rng, 6)
    for dim, blocks in cuts:
        draws = jnp.exp(jax.random.uniform(jax.random.fold_in(own, dim), (blocks,), jnp.float32, smallest / len(cuts), high / len(cuts)))
        loudness = loudness * jnp.repeat(draws, dims[dim] // blocks).reshape([-1 if axis == dim else 1 for axis in range(len(dims))])
    return loudness


def split_up(count, total, most, slope):
    weights = [(1 << 20) // math.isqrt(rank ** slope) + 1 for rank in range(2, count + 1)]
    rest, given = total - most - (count - 1), [1] * (count - 1)
    while rest > 0:
        candidates = [i for i in range(count - 1) if given[i] < most]
        mass, remaining = sum([weights[i] for i in candidates]), rest
        for i in candidates:
            more = min(most - given[i], max(1, remaining * weights[i] // mass), rest)
            given[i] = given[i] + more
            rest = rest - more
    return np.array([most] + given)


def uneven_parts(own_key, amount, total, most, skew):
    if amount == 2:
        one = jax.random.randint(own_key, (), max(1, total - most), min(most, total - 1) + 1)
        return jnp.stack([one, total - one])
    tallies = jnp.asarray(split_up(amount, total, most, skew), jnp.int32)
    couples = (amount - 1) // 2
    donor, receiver = tallies[1:1 + 2 * couples:2], tallies[2:2 + 2 * couples:2]
    room = jnp.minimum(donor - 1, most - receiver)
    shifted = jax.random.randint(jax.random.fold_in(own_key, 1), (couples,), 0, 1 << 20) % (room + 1)
    tallies = tallies.at[1:1 + 2 * couples:2].set(donor - shifted).at[2:2 + 2 * couples:2].set(receiver + shifted)
    return tallies[jax.random.permutation(jax.random.fold_in(own_key, 2), amount)]


def noise(own_key, extent, deviation, reach, cuts=(), held_as=jnp.bfloat16):
    array = jax.random.normal(own_key, extent, jnp.float32) * deviation
    if len(cuts) > 0:
        array = levels(own_key, extent, cuts, -0.22, 0.18) * array
    return jnp.clip(array, min=-reach, max=reach).astype(held_as)


def setup_inputs(seed: int = 0) -> dict:
    streams_of = jax.random.split(jax.random.key(seed), 8)
    return {
        "states": draw_states(jax.random.fold_in(streams_of[7], 71), 0),
        "positions": draw_positions(jax.random.fold_in(streams_of[7], 71), 0),
        "counts": uneven_parts(streams_of[2], DEVICES, TOTAL, CAP, 2).astype(jnp.int32),
        "targets": set_ends(jax.random.randint(streams_of[3], (SLOTS,), 0, VOCAB), jax.random.fold_in(streams_of[3], 1), 0, VOCAB - 1).astype(jnp.int32),
        "table": draw_table(jax.random.fold_in(streams_of[7], 71), 0),
        "h_pre": noise(streams_of[5], (SLOTS, FF), 1.0, 6.0, ((1, 16),)),
        "w_down": noise(streams_of[6], (FF, D), (FF // 64) ** -0.5, 0.375, ((0, 16), (1, 16))),
    }


half_root = 0.7071067811865476
density_scale = 0.3989422804014327


def gelu_slope(inputs):
    return 0.5 * (1.0 + lax.erf(inputs * half_root)) + inputs * jnp.exp(-0.5 * inputs * inputs) * density_scale


def reference(states, positions, counts, targets, table, h_pre, w_down):
    slot_ids = jnp.arange(SLOTS, dtype=jnp.int32)
    owners = (slot_ids // CAP).astype(jnp.int32)
    token_rows = (owners * TOK_DEV + positions).astype(jnp.int32)
    features = jnp.take(states, token_rows, axis=0)
    occupied = (slot_ids % CAP) < jnp.take(counts, owners)
    row_weight = occupied.astype(jnp.float32)
    blocks = 8
    block_rows = VOCAB // blocks
    table_blocks = table.reshape(blocks, block_rows, D)

    def block_logits(table_block):
        return jnp.dot(features, table_block.T, preferred_element_type=jnp.float32)

    logits = lax.map(block_logits, table_blocks)
    largest = jnp.max(logits, axis=(0, 2))
    combined = jnp.sum(jnp.exp(logits - largest[None, :, None]), axis=(0, 2))

    def step(carry, inputs):
        piece, table_block, index = inputs
        softmax = jnp.exp(piece - largest[:, None]) / combined[:, None]
        target_hit = (targets - index * block_rows)[:, None] == jnp.arange(block_rows, dtype=jnp.int32)[None, :]
        dlogits = ((softmax - target_hit.astype(jnp.float32)) * row_weight[:, None]).astype(jnp.bfloat16)
        grad_block = jnp.dot(dlogits.T, features, preferred_element_type=jnp.float32).astype(jnp.bfloat16)
        return carry + jnp.dot(dlogits, table_block, preferred_element_type=jnp.float32), grad_block

    width_grad, grad_blocks = lax.scan(step, jnp.zeros((SLOTS, D), jnp.float32), (logits, table_blocks, jnp.arange(blocks, dtype=jnp.int32)))
    table_grad = grad_blocks.reshape(VOCAB, D)
    grad_rows = width_grad.astype(jnp.bfloat16)
    pre_float = h_pre.astype(jnp.float32)
    activated = jax.nn.gelu(pre_float, approximate=False).astype(jnp.bfloat16)
    w_down_grad = jnp.dot(activated.T, grad_rows, preferred_element_type=jnp.float32)
    hidden = jnp.dot(grad_rows, w_down.T, preferred_element_type=jnp.float32)
    hidden_grad = hidden * gelu_slope(pre_float)
    return table_grad, w_down_grad, hidden_grad
```

```python
import jax
import jax.numpy as jnp
from jax import lax
from jax.sharding import PartitionSpec as P

half_root = 0.7071067811865476
density_scale = 0.3989422804014327
NX, NY, NZ, NC = 4, 4, 8, 2
BOTH = ("dp", "mp")
SLOTS, LIVE, WIDTH, META = 768, 384, 4096, 128
PART = 2176


def spot(x, y, z, c):
    return (y * 4 + z // 2) * 16 + (z % 2) * 8 + x * 2 + c


PLACES = [(x, y, z, c) for x in range(NX) for y in range(NY) for z in range(NZ) for c in range(NC)]


def moved(dx=0, dy=0, dz=0, dc=0):
    return [
        (spot(x, y, z, c), spot((x + dx) % NX, (y + dy) % NY, (z + dz) % NZ, (c + dc) % NC))
        for x, y, z, c in PLACES
    ]


def swapped_z():
    return [(spot(x, y, z, c), spot(x, y, z ^ 1, c)) for x, y, z, c in PLACES]


def send(value, perm):
    return lax.ppermute(value, BOTH, perm)


def gelu_slope(inputs):
    return (
        0.5 * (1.0 + lax.erf(inputs * half_root))
        + inputs * jnp.exp(-0.5 * inputs * inputs) * density_scale
    )


def digits(values):
    return [(values % 256), (values // 256) % 256, values // 65536]


def local(states, positions, counts, targets, table, h_pre, w_down):
    f32, bf16 = jnp.float32, jnp.bfloat16
    dp, mp = lax.axis_index("dp"), lax.axis_index("mp")
    device = dp * 16 + mp
    core, y_at, z_hi = mp % 2, dp // 4, dp % 4

    picked = jnp.take(states, positions, axis=0)
    cap = positions.shape[0]
    order = jnp.arange(cap, dtype=jnp.int32)
    slot_ids = device * cap + order
    live = (order < counts[0]).astype(jnp.int32)
    columns = digits(slot_ids)[:2] + [live] + digits(targets)
    meta = jnp.pad(jnp.stack(columns, axis=1), ((0, 0), (0, META - len(columns)))).astype(bf16)
    rows = jnp.concatenate([picked, meta], axis=1)

    z_groups = [
        [spot(x, y, z, c) for z in range(NZ)]
        for x in range(NX)
        for y in range(NY)
        for c in range(NC)
    ]
    full = WIDTH + META
    spread = jnp.broadcast_to(rows[None], (NZ, cap, full))
    block = lax.all_to_all(spread, BOTH, 0, 0, axis_index_groups=z_groups, tiled=True)
    block = block.reshape(NZ * cap, full)
    left, right = block[:, :PART], block[:, PART:]
    left_y = [left] + [send(left, moved(dy=k)) for k in range(1, NY)]
    right_x = [right] + [send(right, moved(dx=k)) for k in range(1, NX)]
    left = jnp.concatenate(left_y, axis=0)
    right = jnp.concatenate(right_x, axis=0)
    left_xy = [left] + [send(left, moved(dx=k)) for k in range(1, NX)]
    right_yx = [right] + [send(right, moved(dy=k)) for k in range(1, NY)]
    left = jnp.concatenate(left_xy, axis=0)
    small = NZ * cap
    right = jnp.concatenate(
        [right_yx[j][i * small : (i + 1) * small] for i in range(NX) for j in range(NY)], axis=0
    )
    own = jnp.concatenate([left, right], axis=1)
    other = send(own, moved(dc=1))
    gathered = jnp.concatenate([own, other], axis=0)
    features = gathered[:, :WIDTH]
    info = gathered[:, WIDTH : WIDTH + 8].astype(jnp.int32)
    slot_id = info[:, 0] + 256 * info[:, 1]
    alive = info[:, 2]
    labels = info[:, 3] + 256 * info[:, 4] + 65536 * info[:, 5]
    before = (slot_id[None, :] < slot_id[:, None]).astype(jnp.int32) * alive[None, :]
    rank = jnp.where(alive > 0, jnp.sum(before, axis=1), -1)
    ranks = jnp.arange(LIVE, dtype=jnp.int32)
    pick = rank[None, :] == ranks[:, None]
    slot_of_rank = jnp.sum(jnp.where(pick, slot_id[None, :], 0), axis=1)

    vocab_rows = table.shape[0]
    vocab_start = device * vocab_rows
    logits = jnp.einsum("rd,vd->rv", features, table, preferred_element_type=f32)
    top = jnp.max(logits, axis=1)
    total = jnp.sum(jnp.exp(logits - top[:, None]), axis=1)
    stats = jnp.stack(
        [
            jnp.sum(jnp.where(pick, top[None, :], 0.0), axis=1),
            jnp.sum(jnp.where(pick, total[None, :], 0.0), axis=1),
        ]
    )

    def merged(parts):
        largest = jnp.max(parts[:, 0], axis=0)
        return jnp.stack(
            [largest, jnp.sum(parts[:, 1] * jnp.exp(parts[:, 0] - largest[None]), axis=0)]
        )

    stats = merged(jnp.stack([stats, send(stats, moved(dc=1))]))
    chips = [
        [spot(x, y, z, c) for x in range(NX) for y in range(NY) for z in range(NZ)]
        for c in range(NC)
    ]
    stats = merged(
        lax.all_to_all(
            jnp.broadcast_to(stats[None], (128, 2, LIVE)),
            BOTH,
            0,
            0,
            axis_index_groups=chips,
            tiled=True,
        )
    )
    global_top = jnp.sum(jnp.where(pick, stats[0][:, None], 0.0), axis=0)
    global_total = jnp.sum(jnp.where(pick, stats[1][:, None], 0.0), axis=0)
    occupied = (alive > 0)[:, None]
    softmax = jnp.exp(jnp.where(occupied, logits - global_top[:, None], 0.0)) / jnp.where(
        occupied, global_total[:, None], 1.0
    )
    hit = (labels - vocab_start)[:, None] == jnp.arange(vocab_rows, dtype=jnp.int32)[None, :]
    dlogits = jnp.where(occupied, softmax - hit.astype(f32), 0.0).astype(bf16)
    packed = jnp.dot(pick.astype(bf16), dlogits, preferred_element_type=f32).astype(bf16)

    half = LIVE // 2
    mine = lax.dynamic_slice_in_dim(packed, core * half, half, 0)
    theirs = lax.dynamic_slice_in_dim(packed, (1 - core) * half, half, 0)
    away = jnp.dot(theirs, table, preferred_element_type=f32).astype(bf16)
    came = send(away, moved(dc=1))
    width = (jnp.dot(mine, table, preferred_element_type=f32) + came.astype(f32)).astype(bf16)

    def scattered(value, axis, size, at, perm):
        step = value.shape[axis] // size
        cut = lambda k: lax.dynamic_slice_in_dim(value, ((at + k) % size) * step, step, axis)
        parts = [send(cut(k), perm(k)) for k in range(1, size)]
        summed = cut(0).astype(f32)
        for part in parts:
            summed = summed + part.astype(f32)
        return summed

    width = scattered(width, 1, NY, y_at, lambda k: moved(dy=k)).astype(bf16)
    width = scattered(width, 1, 4, z_hi, lambda k: moved(dz=2 * k)).astype(bf16)
    parts = [send(width, moved(dx=k)) for k in range(1, NX)]
    width = sum([p.astype(f32) for p in parts], width.astype(f32)).astype(bf16)
    width = (width.astype(f32) + send(width, swapped_z()).astype(f32)).astype(bf16)
    other_half = send(width, moved(dc=1))
    first = jnp.where(core == 0, width, other_half)
    second = jnp.where(core == 0, other_half, width)
    compact = jnp.concatenate([first, second], axis=0)
    place = (jnp.arange(SLOTS, dtype=jnp.int32)[:, None] == slot_of_rank[None, :]).astype(bf16)
    grad_rows = jnp.dot(place, compact, preferred_element_type=f32).astype(bf16)

    hidden = jnp.einsum("rd,fd->rf", grad_rows, w_down, preferred_element_type=f32).astype(bf16)
    hidden = scattered(hidden, 0, NY, y_at, lambda k: moved(dy=k)).astype(bf16)
    hidden = scattered(hidden, 0, 4, z_hi, lambda k: moved(dz=2 * k))
    block_rows = SLOTS // 16
    own_pre = lax.dynamic_slice_in_dim(h_pre, dp * block_rows, block_rows, 0).astype(f32)
    hidden_grad = hidden * gelu_slope(own_pre)

    table_grad = jnp.einsum(
        "rv,rd->vd", dlogits, features, preferred_element_type=f32
    ).astype(bf16)
    activated = jax.nn.gelu(h_pre.astype(f32), approximate=False).astype(bf16)
    w_down_grad = jnp.einsum("rf,rd->fd", activated, grad_rows, preferred_element_type=f32)
    return (table_grad, w_down_grad, hidden_grad)


def solution(mesh):
    in_specs = (
        P(BOTH, None),
        P(BOTH),
        P(BOTH),
        P(BOTH),
        P(BOTH, None),
        P(None, "mp"),
        P("mp", "dp"),
    )
    out_specs = (P(BOTH, None), P("mp", "dp"), P("dp", "mp"))
    return jax.shard_map(local, mesh=mesh, in_specs=in_specs, out_specs=out_specs, check_vma=False)
```

```python
import functools

import jax
import jax.numpy as jnp
import numpy as np
from jax import lax
from jax.experimental import pallas as pl
from jax.experimental.pallas import tpu as pltpu
from jax.sharding import PartitionSpec as P

half_root = 0.7071067811865476
density_scale = 0.3989422804014327
f32, bf16, i32 = jnp.float32, jnp.bfloat16, jnp.int32
NX, NY, NZ, NC = 4, 4, 8, 2
BOTH = ("dp", "mp")
SLOTS, LIVE, WIDTH, META, VOCAB_ROWS = 768, 384, 4096, 128, 496
HALF, CHUNK, SIDE = LIVE // 2, WIDTH // 4, WIDTH // 2
EMIT = (1, 3, 2, 0)
PARAMS = dict(vmem_limit_bytes=16 * 2**20)
EXACT = lax.Precision.HIGHEST


def spot(x, y, z, c):
    return (y * 4 + z // 2) * 16 + (z % 2) * 8 + x * 2 + c


PLACES = [(x, y, z, c) for x in range(NX) for y in range(NY) for z in range(NZ) for c in range(NC)]


def moved(dx=0, dy=0, dz=0, dc=0):
    return [
        (spot(x, y, z, c), spot((x + dx) % NX, (y + dy) % NY, (z + dz) % NZ, (c + dc) % NC))
        for x, y, z, c in PLACES
    ]


def send(value, perm):
    return lax.ppermute(value, BOTH, perm)


across = moved(dc=1)
z_pair = [(spot(x, y, z, c), spot(x, y, z ^ 1, c)) for x, y, z, c in PLACES]
along_x = {k: moved(dx=k) for k in (1, 3, 2)}
along_y = {k: moved(dy=k) for k in (1, 3, 2)}
along_z = {k: moved(dz=2 * k) for k in (1, 3, 2)}


def rows_dot(a, b, **kw):
    return lax.dot_general(a, b, (((1,), (1,)), ((), ())), preferred_element_type=f32, **kw)


def gelu_slope(inputs):
    return (
        0.5 * (1.0 + lax.erf(inputs * half_root))
        + inputs * jnp.exp(-0.5 * inputs * inputs) * density_scale
    )


def digits(values):
    return [values % 256, (values // 256) % 256, values // 65536]


def one_hot(rank):
    return lax.broadcasted_iota(i32, (LIVE, rank.shape[1]), 0) == rank


def in_vmem(count):
    return [pl.BlockSpec(memory_space=pltpu.VMEM)] * count


def assemble_kernel(*refs):
    *pieces, order, out = refs
    for start in range(0, out.shape[1], 512):
        columns = slice(start, start + 512)
        value = jnp.concatenate([p[:, columns] for p in pieces], axis=0)
        out[:, columns] = jnp.dot(order[...], value, preferred_element_type=f32).astype(bf16)


def stack_kernel(*refs):
    *pieces, out = refs
    height = pieces[0].shape[0]
    for index, piece in enumerate(pieces):
        out[index * height : (index + 1) * height] = piece[...]


def stacked(pieces, order=None):
    extra = [] if order is None else [order]
    rows, columns = pieces[0].shape
    return pl.pallas_call(
        stack_kernel if order is None else assemble_kernel,
        in_specs=in_vmem(len(pieces) + len(extra)),
        out_specs=in_vmem(1)[0],
        out_shape=jax.ShapeDtypeStruct((len(pieces) * rows, columns), bf16),
        compiler_params=pltpu.CompilerParams(**PARAMS),
        cost_estimate=pl.CostEstimate(
            flops=2 * LIVE * LIVE * columns if extra else 0, bytes_accessed=3 << 20, transcendentals=0
        ),
        name="stacked",
    )(*pieces, *extra)


def ranks_kernel(device, meta0, meta1, place0, place1, slots):
    core = device[0] % 2
    pick = (
        lax.broadcasted_iota(i32, (8, META), 0) == lax.broadcasted_iota(i32, (8, META), 1)
    ).astype(bf16)
    rows, keys, lives = [], [], []
    for meta in (meta0[...], meta1[...]):
        rows.append(rows_dot(pick, meta))
        column = meta[:, :3].astype(f32)
        keys.append(column[:, 0:1] + 256.0 * column[:, 1:2])
        lives.append(column[:, 2:3])
    row_keys = [r[0:1] + 256.0 * r[1:2] for r in rows]
    row_lives = [r[2:3] for r in rows]
    shift = (1 - core) * HALF
    lane = lax.broadcasted_iota(i32, (1, LIVE), 1) + core * HALF
    own_rank = jnp.where(lane >= LIVE, lane - LIVE, lane).astype(f32)
    found = jnp.zeros((1, LIVE), f32)
    for side, out in ((0, place0), (1, place1)):
        rank = sum(
            jnp.sum(jnp.where(keys[q] < row_keys[side], lives[q], 0.0), axis=0, keepdims=True)
            for q in range(2)
        )
        alive = row_lives[side] > 0.5
        rank = jnp.where(alive, rank, -1.0).astype(i32)
        turn = rank + shift
        turn = jnp.where(turn >= LIVE, turn - LIVE, turn)
        turn = jnp.where(alive, turn, -1)
        label = [rows[side][k : k + 1].astype(i32) for k in (3, 4, 5)]
        label = label[0] + 256 * label[1] + 65536 * label[2] - device[0] * VOCAB_ROWS
        out[...] = jnp.concatenate([rank, turn, label] + [jnp.zeros_like(rank)] * 5, axis=0)
        down = sum(
            jnp.sum(jnp.where(row_keys[q] < keys[side], row_lives[q], 0.0), axis=1, keepdims=True)
            for q in range(2)
        )
        hit = (down == own_rank) & (lives[side] > 0.5)
        found = found + jnp.sum(jnp.where(hit, keys[side], 0.0), axis=0, keepdims=True)
    slots[...] = found.astype(i32)


def ranks_call(device, left0, left1):
    rows = left0.shape[0]
    meta = pl.BlockSpec((rows, META), lambda i: (0, SIDE // META))
    whole = lambda shape: pl.BlockSpec(shape, lambda i: (0, 0))
    return pl.pallas_call(
        ranks_kernel,
        grid=(1,),
        in_specs=[pl.BlockSpec(memory_space=pltpu.SMEM), meta, meta],
        out_specs=[whole((8, rows)), whole((8, rows)), whole((1, LIVE))],
        out_shape=[jax.ShapeDtypeStruct((8, rows), i32)] * 2
        + [jax.ShapeDtypeStruct((1, LIVE), i32)],
        compiler_params=pltpu.CompilerParams(**PARAMS),
        cost_estimate=pl.CostEstimate(flops=1 << 22, bytes_accessed=1 << 18, transcendentals=0),
        name="ranks",
    )(device, left0, left1)


def logits_kernel(last, *refs):
    if last:
        table, left, right, early, place0, place1, logits, stats = refs
    else:
        table, left, right, logits, stats = refs
    values = rows_dot(table[:, :SIDE], left[:, :SIDE]) + rows_dot(table[:, SIDE:], right[...])
    logits[...] = values
    top = jnp.max(values, axis=0, keepdims=True)
    total = jnp.sum(jnp.exp(values - top), axis=0, keepdims=True)
    found = jnp.concatenate([top, total], axis=0)
    if last:
        stats[...] = rows_dot(
            early[...], one_hot(place0[0:1]).astype(f32), precision=EXACT
        ) + rows_dot(found, one_hot(place1[0:1]).astype(f32), precision=EXACT)
    else:
        stats[...] = found


def logits_call(table, left, right, extra=()):
    vocab, rows = table.shape[0], left.shape[0]
    return pl.pallas_call(
        functools.partial(logits_kernel, bool(extra)),
        in_specs=in_vmem(3 + len(extra)),
        out_specs=in_vmem(2),
        out_shape=[jax.ShapeDtypeStruct((vocab, rows), f32), jax.ShapeDtypeStruct((2, LIVE), f32)],
        compiler_params=pltpu.CompilerParams(**PARAMS),
        cost_estimate=pl.CostEstimate(
            flops=2 * vocab * rows * WIDTH, bytes_accessed=4 << 20, transcendentals=vocab * rows
        ),
        name="logits",
    )(table, left, right, *extra)


def chunk_dot(device, g, value, table):
    y_at, z_hi = device[0] >> 6, (device[0] >> 4) & 3
    parts = []
    for j in range(4):
        start = pl.multiple_of(((y_at + EMIT[g]) & 3) * CHUNK + ((z_hi + j) & 3) * 256, 256)
        parts.append(jnp.dot(value, table[:, pl.ds(start, 256)], preferred_element_type=f32))
    return jnp.concatenate(parts, axis=1)


def dlogits_kernel(device, lg0, lg1, place0, place1, stats, table, *refs):
    (d0, d1, keep), outs = refs[:3], refs[3:7]
    packed = None
    for lg, place, d in ((lg0, place0, d0), (lg1, place1, d1)):
        rank, turn, label = place[0:1], place[1:2], place[2:3]
        where = lax.dot_general(
            stats[...],
            one_hot(rank).astype(f32),
            (((1,), (0,)), ((), ())),
            preferred_element_type=f32,
            precision=EXACT,
        )
        alive = rank >= 0
        top = jnp.where(alive, where[0:1], 0.0)
        total = jnp.where(alive, where[1:2], 1.0)
        values = lg[...]
        soft = jnp.exp(values - top) / total
        hit = lax.broadcasted_iota(i32, values.shape, 0) == label
        grad = jnp.where(alive, soft - jnp.where(hit, 1.0, 0.0), 0.0).astype(bf16)
        d[...] = grad
        part = rows_dot(one_hot(turn).astype(bf16), grad)
        packed = part if packed is None else packed + part
    packed = packed.astype(bf16)
    keep[...] = packed[HALF:]
    theirs = packed[:HALF]
    for g, out in enumerate(outs):
        out[...] = chunk_dot(device, g, theirs, table).astype(bf16)


def dlogits_call(device, logits, places, stats, table):
    vocab = table.shape[0]
    small = [*places, stats]
    out_shapes = [jax.ShapeDtypeStruct((vocab, LIVE), bf16)] * 2
    out_shapes += [jax.ShapeDtypeStruct((HALF, vocab), bf16)]
    out_shapes += [jax.ShapeDtypeStruct((HALF, CHUNK), bf16)] * 4
    return pl.pallas_call(
        dlogits_kernel,
        in_specs=[pl.BlockSpec(memory_space=pltpu.SMEM)] + in_vmem(3 + len(small)),
        out_specs=in_vmem(7),
        out_shape=out_shapes,
        compiler_params=pltpu.CompilerParams(**PARAMS),
        cost_estimate=pl.CostEstimate(
            flops=2 * vocab * HALF * WIDTH, bytes_accessed=4 << 20, transcendentals=vocab * SLOTS
        ),
        name="dlogits",
    )(device, *logits, *small, table)


def own_kernel(device, packed, table, *outs):
    for g, out in enumerate(outs):
        out[...] = chunk_dot(device, g, packed[...], table)


def own_call(device, packed, table):
    vocab = table.shape[0]
    return pl.pallas_call(
        own_kernel,
        in_specs=[pl.BlockSpec(memory_space=pltpu.SMEM)] + in_vmem(2),
        out_specs=in_vmem(4),
        out_shape=[jax.ShapeDtypeStruct((HALF, CHUNK), f32)] * 4,
        compiler_params=pltpu.CompilerParams(**PARAMS),
        cost_estimate=pl.CostEstimate(
            flops=2 * vocab * HALF * WIDTH, bytes_accessed=4 << 20, transcendentals=0
        ),
        name="own_width",
    )(device, packed, table)


def gelu_kernel(device, pre, active, slope):
    values = pre[...].astype(f32)
    active[...] = (0.5 * values * (1.0 + lax.erf(values * half_root))).astype(bf16)

    @pl.when(pl.program_id(0) == device[0] >> 6)
    def _():
        start = pl.multiple_of(((device[0] >> 4) & 3) * 48, 16)
        slope[...] = gelu_slope(pre[pl.ds(start, 48), :].astype(f32))


def gelu_call(device, pre):
    rows, units = pre.shape
    block = pl.BlockSpec((rows // 4, units), lambda i: (i, 0))
    return pl.pallas_call(
        gelu_kernel,
        grid=(4,),
        in_specs=[pl.BlockSpec(memory_space=pltpu.SMEM), block],
        out_specs=[block, pl.BlockSpec((48, units), lambda i: (0, 0))],
        out_shape=[
            jax.ShapeDtypeStruct((rows, units), bf16),
            jax.ShapeDtypeStruct((48, units), f32),
        ],
        compiler_params=pltpu.CompilerParams(**PARAMS),
        cost_estimate=pl.CostEstimate(
            flops=rows * units * 30, bytes_accessed=rows * units * 4, transcendentals=rows * units
        ),
        name="gelu",
    )(device, pre)


def hidden_kernel(device, own, other, slots, down, rows, *outs):
    y_at, z_hi = device[0] >> 6, (device[0] >> 4) & 3
    place = lax.broadcasted_iota(i32, (SLOTS, LIVE), 0) == slots[...]
    compact = jnp.concatenate([own[...], other[...]], axis=0)
    rows[...] = jnp.dot(place.astype(bf16), compact, preferred_element_type=f32).astype(bf16)
    for k, out in zip(EMIT, outs):
        parts = []
        for j in range(4):
            start = ((y_at + k) & 3) * 192 + ((z_hi + j) & 3) * 48
            parts.append(rows[pl.ds(pl.multiple_of(start, 16), 48), :])
        out[...] = rows_dot(jnp.concatenate(parts, axis=0), down[...]).astype(out.dtype)


def hidden_call(device, own, other, slots, down):
    shapes = [jax.ShapeDtypeStruct((SLOTS, own.shape[1]), bf16)]
    shapes += [jax.ShapeDtypeStruct((192, down.shape[0]), f32 if k == 0 else bf16) for k in EMIT]
    return pl.pallas_call(
        hidden_kernel,
        in_specs=[pl.BlockSpec(memory_space=pltpu.SMEM)] + in_vmem(4),
        out_specs=in_vmem(len(shapes)),
        out_shape=shapes,
        compiler_params=pltpu.CompilerParams(**PARAMS),
        cost_estimate=pl.CostEstimate(flops=10**9, bytes_accessed=4 << 20, transcendentals=0),
        name="hidden",
    )(device, own, other, slots, down)


def table_grad_kernel(d0, d1, l0, l1, r0, r1, out):
    j = pl.program_id(0)

    @pl.when(j < 2)
    def _():
        out[...] = (
            jnp.dot(d0[...], l0[...], preferred_element_type=f32)
            + jnp.dot(d1[...], l1[...], preferred_element_type=f32)
        ).astype(bf16)

    @pl.when(j >= 2)
    def _():
        out[...] = (
            jnp.dot(d0[...], r0[...], preferred_element_type=f32)
            + jnp.dot(d1[...], r1[...], preferred_element_type=f32)
        ).astype(bf16)


def table_grad_call(d0, d1, l0, l1, r0, r1):
    vocab, rows = d0.shape
    whole = pl.BlockSpec((vocab, rows), lambda j: (0, 0))
    left = pl.BlockSpec((rows, CHUNK), lambda j: (0, jnp.minimum(j, 1)))
    right = pl.BlockSpec((rows, CHUNK), lambda j: (0, jnp.maximum(j - 2, 0)))
    return pl.pallas_call(
        table_grad_kernel,
        grid=(4,),
        in_specs=[whole, whole, left, left, right, right],
        out_specs=pl.BlockSpec((vocab, CHUNK), lambda j: (0, j)),
        out_shape=jax.ShapeDtypeStruct((vocab, WIDTH), bf16),
        compiler_params=pltpu.CompilerParams(**PARAMS),
        cost_estimate=pl.CostEstimate(
            flops=4 * vocab * rows * WIDTH, bytes_accessed=12 << 20, transcendentals=0
        ),
        name="table_grad",
    )(d0, d1, l0, l1, r0, r1)


def local(states, positions, counts, targets, table, h_pre, w_down):
    dp, mp = lax.axis_index("dp"), lax.axis_index("mp")
    device = dp * 16 + mp
    where = device.astype(i32)[None]

    picked = states.at[positions].get(mode="promise_in_bounds")
    cap = positions.shape[0]
    order = jnp.arange(cap, dtype=i32)
    live = (order < counts[0]).astype(i32)
    columns = digits(device * cap + order)[:2] + [live] + digits(targets)
    meta = jnp.pad(jnp.stack(columns, axis=1), ((0, 0), (0, META - len(columns)))).astype(bf16)
    rows = jnp.concatenate([picked[:, :SIDE], meta, picked[:, SIDE:]], axis=1)

    z_groups = [
        [spot(x, y, z, c) for z in range(NZ)]
        for x in range(NX)
        for y in range(NY)
        for c in range(NC)
    ]
    full = WIDTH + META
    spread = jnp.broadcast_to(rows[None], (NZ, cap, full))
    block = lax.all_to_all(spread, BOTH, 0, 0, axis_index_groups=z_groups, tiled=True)
    small = NZ * cap
    block = block.reshape(small, full)
    part = SIDE + META
    left, right = block[:, :part], block[:, part:]

    def collect(value, along):
        got = {0: value, **{k: send(value, along[k]) for k in (1, 3, 2)}}
        return [got[k] for k in range(4)]

    left = jnp.concatenate(collect(left, along_y), axis=0)
    right = jnp.concatenate(collect(right, along_x), axis=0)
    left, right = lax.optimization_barrier((left, right))
    left0 = stacked(collect(left, along_x))
    left1 = send(left0, across)
    source = np.arange(LIVE).reshape(NY, NX, small).transpose(1, 0, 2).reshape(-1)
    reorder = jnp.asarray(source[:, None] == np.arange(LIVE)[None, :], bf16)
    right0 = stacked(collect(right, along_y), reorder)
    right1 = send(right0, across)

    *places, slot_of = ranks_call(where, left0, left1)
    logits0, early = logits_call(table, left0, right0)
    logits1, stats = logits_call(table, left1, right1, (early, *places))

    def merged(parts):
        largest = functools.reduce(jnp.maximum, [p[0] for p in parts])
        return jnp.stack([largest, sum(p[1] * jnp.exp(p[0] - largest) for p in parts)])

    stats = merged([stats, send(stats, across)])
    stats = merged(collect(stats, along_x))
    stats = merged(collect(stats, along_y))
    stats = merged([stats, send(stats, z_pair)])
    stats = merged(collect(stats, along_z))

    d0, d1, keep, *away = dlogits_call(
        where, (logits0, logits1), places, stats, table
    )
    keep, h_pre = lax.optimization_barrier((keep, h_pre))
    activated, slope = gelu_call(where, h_pre)
    came = [send(a, across) for a in away]
    mine = own_call(where, keep, table)
    sums = [m + c.astype(f32) for m, c in zip(mine, came)]

    def scattered(chunks, along, axis):
        sent = [send(chunks[k].astype(bf16), along[k]) for k in (1, 3, 2)]
        return chunks[0], sent

    def total(own, parts):
        return sum([p.astype(f32) for p in parts], own)

    chunks = {k: sums[g] for g, k in enumerate(EMIT)}
    own, parts = scattered(chunks, along_y, 1)
    quarter = CHUNK // 4
    cut = lambda a, j: a[:, j * quarter : (j + 1) * quarter]
    chunks = {j: total(cut(own, j), [cut(p, j) for p in parts]) for j in range(4)}
    own, parts = scattered(chunks, along_z, 1)
    width = total(own, parts)
    width = sum(collect(width, along_x))
    width = width + send(width, z_pair)
    width = width.astype(bf16)
    grad_rows, *chunks = hidden_call(where, width, send(width, across), slot_of, w_down)
    chunks = dict(zip(EMIT, chunks))
    block_rows = SLOTS // 16
    own, parts = scattered(chunks, along_y, 0)
    cut = lambda a, j: a[j * block_rows : (j + 1) * block_rows]
    chunks = {j: total(cut(own, j), [cut(p, j) for p in parts]) for j in range(4)}
    own, parts = scattered(chunks, along_z, 0)
    hidden_grad = total(own, parts) * slope

    table_grad = table_grad_call(d0, d1, left0, left1, right0, right1)
    w_down_grad = jnp.einsum("rf,rd->fd", activated, grad_rows, preferred_element_type=f32)
    return (table_grad, w_down_grad, hidden_grad)


def solution(mesh):
    in_specs = (
        P(BOTH, None),
        P(BOTH),
        P(BOTH),
        P(BOTH),
        P(BOTH, None),
        P(None, "mp"),
        P("mp", "dp"),
    )
    out_specs = (P(BOTH, None), P("mp", "dp"), P("dp", "mp"))
    return jax.shard_map(local, mesh=mesh, in_specs=in_specs, out_specs=out_specs, check_vma=False)
```

```python
import functools

import jax
import jax.numpy as jnp
import numpy as np
from jax import lax
from jax.experimental import pallas as pl
from jax.experimental.pallas import tpu as pltpu
from jax.sharding import PartitionSpec as P

half_root = 0.7071067811865476
density_scale = 0.3989422804014327
f32, bf16, i32 = jnp.float32, jnp.bfloat16, jnp.int32
NX, NY, NZ, NC = 4, 4, 8, 2
BOTH = ("dp", "mp")
SLOTS, LIVE, WIDTH, META, VOCAB_ROWS = 768, 384, 4096, 128, 496
HALF, CHUNK, SIDE = LIVE // 2, WIDTH // 4, WIDTH // 2
EMIT = (1, 3, 2, 0)
PARAMS = dict(vmem_limit_bytes=16 * 2**20)
EXACT = lax.Precision.HIGHEST


def spot(x, y, z, c):
    return (y * 4 + z // 2) * 16 + (z % 2) * 8 + x * 2 + c


PLACES = [(x, y, z, c) for x in range(NX) for y in range(NY) for z in range(NZ) for c in range(NC)]


def send(value, perm):
    return lax.ppermute(value, BOTH, perm)


def crossed(mx=0, my=0, mz=0, mc=0):
    return [(spot(x, y, z, c), spot(x ^ mx, y ^ my, z ^ mz, c ^ mc)) for x, y, z, c in PLACES]


across, z_pair = crossed(mc=1), crossed(mz=1)
along_x = {k: crossed(mx=k) for k in (1, 3, 2)}
along_y = {k: crossed(my=k) for k in (1, 3, 2)}
along_z = {k: crossed(mz=2 * k) for k in (1, 3, 2)}


def by_core(zero, one):
    return {k: [p for p in zero[k] if p[0] % 2 == 0] + [p for p in one[k] if p[0] % 2] for k in (1, 3, 2)}


first, second = by_core(along_y, along_z), by_core(along_z, along_y)


def dp_place(device, core, k, j):
    y_at, z_hi = device[0] >> 6, (device[0] >> 4) & 3
    return y_at ^ jnp.where(core == 0, k, j), z_hi ^ jnp.where(core == 0, j, k)


def rows_dot(a, b, **kw):
    return lax.dot_general(a, b, (((1,), (1,)), ((), ())), preferred_element_type=f32, **kw)


def gelu_slope(inputs):
    return (
        0.5 * (1.0 + lax.erf(inputs * half_root))
        + inputs * jnp.exp(-0.5 * inputs * inputs) * density_scale
    )


def digits(values):
    return [values % 256, (values // 256) % 256, values // 65536]


def one_hot(rank):
    return lax.broadcasted_iota(i32, (LIVE, rank.shape[1]), 0) == rank


def in_vmem(count):
    return [pl.BlockSpec(memory_space=pltpu.VMEM)] * count


def assemble_kernel(*refs):
    *pieces, order, out = refs
    for start in range(0, out.shape[1], 512):
        columns = slice(start, start + 512)
        value = jnp.concatenate([p[:, columns] for p in pieces], axis=0)
        out[:, columns] = jnp.dot(order[...], value, preferred_element_type=f32).astype(bf16)


def stack_kernel(*refs):
    *pieces, out = refs
    start = 0
    for piece in pieces:
        out[start : start + piece.shape[0]] = piece[...]
        start += piece.shape[0]


def stacked(pieces, order=None):
    extra = [] if order is None else [order]
    rows, columns = sum(p.shape[0] for p in pieces), pieces[0].shape[1]
    return pl.pallas_call(
        stack_kernel if order is None else assemble_kernel,
        in_specs=in_vmem(len(pieces) + len(extra)),
        out_specs=in_vmem(1)[0],
        out_shape=jax.ShapeDtypeStruct((rows, columns), bf16),
        compiler_params=pltpu.CompilerParams(**PARAMS),
        cost_estimate=pl.CostEstimate(
            flops=2 * LIVE * LIVE * columns if extra else 0, bytes_accessed=3 << 20, transcendentals=0
        ),
        name="stacked",
    )(*pieces, *extra)


def prepare_kernel(device, positions, counts, targets, states, out):
    cap = out.shape[1]
    row = lax.broadcasted_iota(i32, (8, META), 0)
    lane = lax.broadcasted_iota(i32, (8, META), 1)
    token, fields = jnp.full((8, META), -1, i32), jnp.zeros((8, META), i32)
    for s in range(cap):
        slot, target = device[0] * cap + s, targets[s]
        values = (
            slot & 255,
            slot >> 8,
            jnp.where(s < counts[0], 1, 0),
            target & 255,
            (target >> 8) & 255,
            target >> 16,
        )
        token = jnp.where(row == s, positions[s], token)
        for index, value in enumerate(values):
            fields = jnp.where((row == s) & (lane == index), value, fields)
    pick = (token == lane).astype(bf16)
    meta = fields.astype(f32).astype(bf16)
    rows = jnp.dot(pick, states[...], preferred_element_type=f32).astype(bf16)
    for z in range(NZ):
        out[z, :, :SIDE] = rows[:cap, :SIDE]
        out[z, :, SIDE : SIDE + META] = meta[:cap]
        out[z, :, SIDE + META :] = rows[:cap, SIDE:]


def prepare_call(device, positions, counts, targets, states):
    return pl.pallas_call(
        prepare_kernel,
        in_specs=[pl.BlockSpec(memory_space=pltpu.SMEM)] * 4 + in_vmem(1),
        out_specs=in_vmem(1)[0],
        out_shape=jax.ShapeDtypeStruct((NZ, positions.shape[0], WIDTH + META), bf16),
        compiler_params=pltpu.CompilerParams(**PARAMS),
        name="prepare",
    )(device, positions, counts, targets, states)


def ranks_kernel(device, meta0, meta1, place0, place1, slots):
    core = device[0] % 2
    pick = (
        lax.broadcasted_iota(i32, (8, META), 0) == lax.broadcasted_iota(i32, (8, META), 1)
    ).astype(bf16)
    rows, keys, lives = [], [], []
    for meta in (meta0[...], meta1[...]):
        rows.append(rows_dot(pick, meta))
        column = meta[:, :3].astype(f32)
        keys.append(column[:, 0:1] + 256.0 * column[:, 1:2])
        lives.append(column[:, 2:3])
    row_keys = [r[0:1] + 256.0 * r[1:2] for r in rows]
    row_lives = [r[2:3] for r in rows]
    shift = (1 - core) * HALF
    lane = lax.broadcasted_iota(i32, (1, LIVE), 1) + core * HALF
    own_rank = jnp.where(lane >= LIVE, lane - LIVE, lane).astype(f32)
    found = jnp.zeros((1, LIVE), f32)
    for side, out in ((0, place0), (1, place1)):
        rank = sum(
            jnp.sum(jnp.where(keys[q] < row_keys[side], lives[q], 0.0), axis=0, keepdims=True)
            for q in range(2)
        )
        alive = row_lives[side] > 0.5
        rank = jnp.where(alive, rank, -1.0).astype(i32)
        turn = rank + shift
        turn = jnp.where(turn >= LIVE, turn - LIVE, turn)
        turn = jnp.where(alive, turn, -1)
        label = [rows[side][k : k + 1].astype(i32) for k in (3, 4, 5)]
        label = label[0] + 256 * label[1] + 65536 * label[2] - device[0] * VOCAB_ROWS
        out[...] = jnp.concatenate([rank, turn, label] + [jnp.zeros_like(rank)] * 5, axis=0)
        down = sum(
            jnp.sum(jnp.where(row_keys[q] < keys[side], row_lives[q], 0.0), axis=1, keepdims=True)
            for q in range(2)
        )
        hit = (down == own_rank) & (lives[side] > 0.5)
        found = found + jnp.sum(jnp.where(hit, keys[side], 0.0), axis=0, keepdims=True)
    slots[...] = found.astype(i32)


def ranks_call(device, left0, left1):
    rows = left0.shape[0]
    meta = pl.BlockSpec((rows, META), lambda i: (0, SIDE // META))
    whole = lambda shape: pl.BlockSpec(shape, lambda i: (0, 0))
    return pl.pallas_call(
        ranks_kernel,
        grid=(1,),
        in_specs=[pl.BlockSpec(memory_space=pltpu.SMEM), meta, meta],
        out_specs=[whole((8, rows)), whole((8, rows)), whole((1, LIVE))],
        out_shape=[jax.ShapeDtypeStruct((8, rows), i32)] * 2
        + [jax.ShapeDtypeStruct((1, LIVE), i32)],
        compiler_params=pltpu.CompilerParams(**PARAMS),
        cost_estimate=pl.CostEstimate(flops=1 << 22, bytes_accessed=1 << 18, transcendentals=0),
        name="ranks",
    )(device, left0, left1)


def logits_kernel(last, *refs):
    if last:
        table, left, right, early, place0, place1, logits, stats = refs
    else:
        table, left, right, logits, stats = refs
    values = rows_dot(table[:, :SIDE], left[:, :SIDE]) + rows_dot(table[:, SIDE:], right[...])
    logits[...] = values
    top = jnp.max(values, axis=0, keepdims=True)
    total = jnp.sum(jnp.exp(values - top), axis=0, keepdims=True)
    found = jnp.concatenate([top, total], axis=0)
    if last:
        stats[...] = rows_dot(
            early[...], one_hot(place0[0:1]).astype(f32), precision=EXACT
        ) + rows_dot(found, one_hot(place1[0:1]).astype(f32), precision=EXACT)
    else:
        stats[...] = found


def logits_call(table, left, right, extra=()):
    vocab, rows = table.shape[0], left.shape[0]
    return pl.pallas_call(
        functools.partial(logits_kernel, bool(extra)),
        in_specs=in_vmem(3 + len(extra)),
        out_specs=in_vmem(2),
        out_shape=[jax.ShapeDtypeStruct((vocab, rows), f32), jax.ShapeDtypeStruct((2, LIVE), f32)],
        compiler_params=pltpu.CompilerParams(**PARAMS),
        cost_estimate=pl.CostEstimate(
            flops=2 * vocab * rows * WIDTH, bytes_accessed=4 << 20, transcendentals=vocab * rows
        ),
        name="logits",
    )(table, left, right, *extra)


def chunk_dot(device, core, g, value, table):
    parts = []
    for j in range(4):
        y_to, z_to = dp_place(device, core, EMIT[g], j)
        start = pl.multiple_of(y_to * CHUNK + z_to * 256, 256)
        parts.append(jnp.dot(value, table[:, pl.ds(start, 256)], preferred_element_type=f32))
    return jnp.concatenate(parts, axis=1)


def dlogits_kernel(device, lg0, lg1, place0, place1, stats, table, *refs):
    (d0, d1, keep), outs = refs[:3], refs[3:7]
    packed = None
    for lg, place, d in ((lg0, place0, d0), (lg1, place1, d1)):
        rank, turn, label = place[0:1], place[1:2], place[2:3]
        where = lax.dot_general(
            stats[...],
            one_hot(rank).astype(f32),
            (((1,), (0,)), ((), ())),
            preferred_element_type=f32,
            precision=EXACT,
        )
        alive = rank >= 0
        top = jnp.where(alive, where[0:1], 0.0)
        total = jnp.where(alive, where[1:2], 1.0)
        values = lg[...]
        soft = jnp.exp(values - top) / total
        hit = lax.broadcasted_iota(i32, values.shape, 0) == label
        grad = jnp.where(alive, soft - jnp.where(hit, 1.0, 0.0), 0.0).astype(bf16)
        d[...] = grad
        part = rows_dot(one_hot(turn).astype(bf16), grad)
        packed = part if packed is None else packed + part
    packed = packed.astype(bf16)
    keep[...] = packed[HALF:]
    theirs = packed[:HALF]
    for g, out in enumerate(outs):
        out[...] = chunk_dot(device, 1 - (device[0] & 1), g, theirs, table).astype(bf16)


def dlogits_call(device, logits, places, stats, table):
    vocab = table.shape[0]
    small = [*places, stats]
    out_shapes = [jax.ShapeDtypeStruct((vocab, LIVE), bf16)] * 2
    out_shapes += [jax.ShapeDtypeStruct((HALF, vocab), bf16)]
    out_shapes += [jax.ShapeDtypeStruct((HALF, CHUNK), bf16)] * 4
    return pl.pallas_call(
        dlogits_kernel,
        in_specs=[pl.BlockSpec(memory_space=pltpu.SMEM)] + in_vmem(3 + len(small)),
        out_specs=in_vmem(7),
        out_shape=out_shapes,
        compiler_params=pltpu.CompilerParams(**PARAMS),
        cost_estimate=pl.CostEstimate(
            flops=2 * vocab * HALF * WIDTH, bytes_accessed=4 << 20, transcendentals=vocab * SLOTS
        ),
        name="dlogits",
    )(device, *logits, *small, table)


def own_kernel(device, packed, table, *outs):
    for g, out in enumerate(outs):
        out[...] = chunk_dot(device, device[0] & 1, g, packed[...], table)


def own_call(device, packed, table):
    vocab = table.shape[0]
    return pl.pallas_call(
        own_kernel,
        in_specs=[pl.BlockSpec(memory_space=pltpu.SMEM)] + in_vmem(2),
        out_specs=in_vmem(4),
        out_shape=[jax.ShapeDtypeStruct((HALF, CHUNK), f32)] * 4,
        compiler_params=pltpu.CompilerParams(**PARAMS),
        cost_estimate=pl.CostEstimate(
            flops=2 * vocab * HALF * WIDTH, bytes_accessed=4 << 20, transcendentals=0
        ),
        name="own_width",
    )(device, packed, table)


def gelu_kernel(device, pre, active, slope):
    values = pre[...].astype(f32)
    active[...] = (0.5 * values * (1.0 + lax.erf(values * half_root))).astype(bf16)

    @pl.when(pl.program_id(0) == device[0] >> 6)
    def _():
        start = pl.multiple_of(((device[0] >> 4) & 3) * 48, 16)
        slope[...] = gelu_slope(pre[pl.ds(start, 48), :].astype(f32))


def gelu_call(device, pre):
    rows, units = pre.shape
    block = pl.BlockSpec((rows // 4, units), lambda i: (i, 0))
    return pl.pallas_call(
        gelu_kernel,
        grid=(4,),
        in_specs=[pl.BlockSpec(memory_space=pltpu.SMEM), block],
        out_specs=[block, pl.BlockSpec((48, units), lambda i: (0, 0))],
        out_shape=[
            jax.ShapeDtypeStruct((rows, units), bf16),
            jax.ShapeDtypeStruct((48, units), f32),
        ],
        compiler_params=pltpu.CompilerParams(**PARAMS),
        cost_estimate=pl.CostEstimate(
            flops=rows * units * 30, bytes_accessed=rows * units * 4, transcendentals=rows * units
        ),
        name="gelu",
    )(device, pre)


def hidden_kernel(device, own, other, slots, down, rows, *outs):
    place = lax.broadcasted_iota(i32, (SLOTS, LIVE), 0) == slots[...]
    compact = jnp.concatenate([own[...], other[...]], axis=0)
    rows[...] = jnp.dot(place.astype(bf16), compact, preferred_element_type=f32).astype(bf16)
    for k, out in zip(EMIT, outs):
        parts = []
        for j in range(4):
            y_to, z_to = dp_place(device, device[0] & 1, k, j)
            start = y_to * 192 + z_to * 48
            parts.append(rows[pl.ds(pl.multiple_of(start, 16), 48), :])
        out[...] = rows_dot(jnp.concatenate(parts, axis=0), down[...]).astype(out.dtype)


def hidden_call(device, own, other, slots, down):
    shapes = [jax.ShapeDtypeStruct((SLOTS, own.shape[1]), bf16)]
    shapes += [jax.ShapeDtypeStruct((192, down.shape[0]), f32 if k == 0 else bf16) for k in EMIT]
    return pl.pallas_call(
        hidden_kernel,
        in_specs=[pl.BlockSpec(memory_space=pltpu.SMEM)] + in_vmem(4),
        out_specs=in_vmem(len(shapes)),
        out_shape=shapes,
        compiler_params=pltpu.CompilerParams(**PARAMS),
        cost_estimate=pl.CostEstimate(flops=10**9, bytes_accessed=4 << 20, transcendentals=0),
        name="hidden",
    )(device, own, other, slots, down)


def table_grad_kernel(d0, d1, l0, l1, r0, r1, out):
    j = pl.program_id(0)

    @pl.when(j < 2)
    def _():
        out[...] = (
            jnp.dot(d0[...], l0[...], preferred_element_type=f32)
            + jnp.dot(d1[...], l1[...], preferred_element_type=f32)
        ).astype(bf16)

    @pl.when(j >= 2)
    def _():
        out[...] = (
            jnp.dot(d0[...], r0[...], preferred_element_type=f32)
            + jnp.dot(d1[...], r1[...], preferred_element_type=f32)
        ).astype(bf16)


def table_grad_call(d0, d1, l0, l1, r0, r1):
    vocab, rows = d0.shape
    whole = pl.BlockSpec((vocab, rows), lambda j: (0, 0))
    left = pl.BlockSpec((rows, CHUNK), lambda j: (0, jnp.minimum(j, 1)))
    right = pl.BlockSpec((rows, CHUNK), lambda j: (0, jnp.maximum(j - 2, 0)))
    return pl.pallas_call(
        table_grad_kernel,
        grid=(4,),
        in_specs=[whole, whole, left, left, right, right],
        out_specs=pl.BlockSpec((vocab, CHUNK), lambda j: (0, j)),
        out_shape=jax.ShapeDtypeStruct((vocab, WIDTH), bf16),
        compiler_params=pltpu.CompilerParams(**PARAMS),
        cost_estimate=pl.CostEstimate(
            flops=4 * vocab * rows * WIDTH, bytes_accessed=12 << 20, transcendentals=0
        ),
        name="table_grad",
    )(d0, d1, l0, l1, r0, r1)


def local(states, positions, counts, targets, table, h_pre, w_down):
    dp, mp = lax.axis_index("dp"), lax.axis_index("mp")
    device = dp * 16 + mp
    where = device.astype(i32)[None]

    spread = prepare_call(where, positions, counts, targets, states)
    cap = positions.shape[0]
    z_groups = [
        [spot(x, y, z, c) for z in range(NZ)]
        for x in range(NX)
        for y in range(NY)
        for c in range(NC)
    ]
    full = WIDTH + META
    block = lax.all_to_all(spread, BOTH, 0, 0, axis_index_groups=z_groups, tiled=True)
    small = NZ * cap
    block = block.reshape(small, full)
    part = SIDE + META
    left, right = block[:, :part], block[:, part:]

    def collect(value, along):
        got = {0: value, **{k: send(value, along[k]) for k in (1, 3, 2)}}
        return [got[k] for k in range(4)]

    left = jnp.concatenate(collect(left, along_y), axis=0)
    right = jnp.concatenate(collect(right, along_x), axis=0)
    left, right = lax.optimization_barrier((left, right))
    lefts, rights = {0: left}, {0: right}
    for k in (1, 3, 2):
        if k == 2:
            right, lefts[1] = lax.optimization_barrier((right, lefts[1]))
        lefts[k] = send(left, along_x[k])
        rights[k] = send(right, along_y[k])
    left0 = stacked([lefts[k] for k in range(4)])
    left1 = send(left0, across)
    source = np.arange(LIVE).reshape(NY, NX, small).transpose(1, 0, 2).reshape(-1)
    reorder = jnp.asarray(source[:, None] == np.arange(LIVE)[None, :], bf16)
    right0 = stacked([rights[k] for k in range(4)], reorder)
    right1 = send(right0, across)

    *places, slot_of = ranks_call(where, left0, left1)
    logits0, early = logits_call(table, left0, right0)
    logits1, stats = logits_call(table, left1, right1, (early, *places))

    def merged(parts):
        largest = functools.reduce(jnp.maximum, [p[0] for p in parts])
        return jnp.stack([largest, sum(p[1] * jnp.exp(p[0] - largest) for p in parts)])

    stats = merged([stats, send(stats, across)])
    stats = merged(collect(stats, along_x))
    stats = merged(collect(stats, along_y))
    stats = merged([stats, send(stats, z_pair)])
    stats = merged(collect(stats, along_z))

    d0, d1, keep, *away = dlogits_call(
        where, (logits0, logits1), places, stats, table
    )
    keep, h_pre = lax.optimization_barrier((keep, h_pre))
    activated, slope = gelu_call(where, h_pre)
    came = [send(a, across) for a in away]
    mine = own_call(where, keep, table)
    sums = [m + c.astype(f32) for m, c in zip(mine, came)]

    def scattered(chunks, along):
        return chunks[0], [send(chunks[k].astype(bf16), along[k]) for k in (1, 3, 2)]

    def total(own, parts):
        return sum([p.astype(f32) for p in parts], own)

    def relayed(own, one, three, two):
        half = own.shape[0] // 2
        low, high = slice(0, half), slice(half, None)
        via_one = send(two[low].astype(bf16), first[1])
        via_three = send(two[high].astype(bf16), first[3])
        plain_one = send(one[low].astype(bf16), first[1])
        plain_three = send(three[high].astype(bf16), first[3])
        joined_three = (three[low].astype(f32) + via_one.astype(f32)).astype(bf16)
        joined_one = (one[high].astype(f32) + via_three.astype(f32)).astype(bf16)
        joined_three = send(joined_three, first[3])
        joined_one = send(joined_one, first[1])
        return (
            total(own[low], [plain_one, joined_three]),
            total(own[high], [joined_one, plain_three]),
        )

    chunks = {k: sums[g] for g, k in enumerate(EMIT)}
    halves = relayed(chunks[0], chunks[1], chunks[3], chunks[2])
    quarter = CHUNK // 4
    chunks = {
        j: jnp.concatenate([h[:, j * quarter : (j + 1) * quarter] for h in halves], axis=0)
        for j in range(4)
    }
    own, parts = scattered(chunks, second)
    width = total(own, parts)
    narrow = width.astype(bf16)
    width = total(width, [send(narrow, along_x[k]) for k in (1, 3, 2)])
    width = width + send(width, z_pair)
    width = width.astype(bf16)
    grad_rows, *chunks = hidden_call(where, width, send(width, across), slot_of, w_down)
    chunks = dict(zip(EMIT, chunks))
    block_rows = SLOTS // 16
    low, high = relayed(chunks[0], chunks[1], chunks[3], chunks[2])
    chunks = {j: (low, high)[j // 2][j % 2 * block_rows :][:block_rows] for j in range(4)}
    own, parts = scattered(chunks, second)
    hidden_grad = total(own, parts) * slope

    table_grad = table_grad_call(d0, d1, left0, left1, right0, right1)
    w_down_grad = jnp.einsum("rf,rd->fd", activated, grad_rows, preferred_element_type=f32)
    return (table_grad, w_down_grad, hidden_grad)


def solution(mesh):
    in_specs = (
        P(BOTH, None),
        P(BOTH),
        P(BOTH),
        P(BOTH),
        P(BOTH, None),
        P(None, "mp"),
        P("mp", "dp"),
    )
    out_specs = (P(BOTH, None), P("mp", "dp"), P("dp", "mp"))
    return jax.shard_map(local, mesh=mesh, in_specs=in_specs, out_specs=out_specs, check_vma=False)
```

```python
import functools

import jax
import jax.numpy as jnp
import numpy as np
from jax import lax
from jax.experimental import pallas as pl
from jax.experimental.pallas import tpu as pltpu
from jax.sharding import PartitionSpec as P

half_root = 0.7071067811865476
density_scale = 0.3989422804014327
f32, bf16, i32 = jnp.float32, jnp.bfloat16, jnp.int32
NX, NY, NZ, NC = 4, 4, 8, 2
BOTH = ("dp", "mp")
SLOTS, LIVE, WIDTH, META, VOCAB_ROWS = 768, 384, 4096, 128, 496
HALF, CHUNK, SIDE = LIVE // 2, WIDTH // 4, WIDTH // 2
EMIT = (1, 3, 2, 0)
PARAMS = dict(vmem_limit_bytes=16 * 2**20)
EXACT = lax.Precision.HIGHEST


def spot(x, y, z, c):
    return (y * 4 + z // 2) * 16 + (z % 2) * 8 + x * 2 + c


PLACES = [(x, y, z, c) for x in range(NX) for y in range(NY) for z in range(NZ) for c in range(NC)]


def send(value, perm):
    return lax.ppermute(value, BOTH, perm)


def crossed(mx=0, my=0, mz=0, mc=0):
    return [(spot(x, y, z, c), spot(x ^ mx, y ^ my, z ^ mz, c ^ mc)) for x, y, z, c in PLACES]


across, z_pair = crossed(mc=1), crossed(mz=1)
along_x = {k: crossed(mx=k) for k in (1, 3, 2)}
along_y = {k: crossed(my=k) for k in (1, 3, 2)}
along_z = {k: crossed(mz=2 * k) for k in (1, 3, 2)}


def by_core(zero, one):
    return {k: [p for p in zero[k] if p[0] % 2 == 0] + [p for p in one[k] if p[0] % 2] for k in (1, 3, 2)}


first, second = by_core(along_y, along_z), by_core(along_z, along_y)


def dp_place(device, core, k, j):
    y_at, z_hi = device[0] >> 6, (device[0] >> 4) & 3
    return y_at ^ jnp.where(core == 0, k, j), z_hi ^ jnp.where(core == 0, j, k)


def rows_dot(a, b, **kw):
    return lax.dot_general(a, b, (((1,), (1,)), ((), ())), preferred_element_type=f32, **kw)


def gelu_slope(inputs):
    return (
        0.5 * (1.0 + lax.erf(inputs * half_root))
        + inputs * jnp.exp(-0.5 * inputs * inputs) * density_scale
    )


def digits(values):
    return [values % 256, (values // 256) % 256, values // 65536]


def one_hot(rank):
    return lax.broadcasted_iota(i32, (LIVE, rank.shape[1]), 0) == rank


def in_vmem(count):
    return [pl.BlockSpec(memory_space=pltpu.VMEM)] * count


def anywhere(count):
    return [pl.BlockSpec(memory_space=pl.ANY)] * count


def stack_kernel(spots, turned, *refs):
    *pieces, out = refs
    for (index, sub), piece in zip(spots, pieces):
        for row in range(0, piece.shape[0], 48):
            start = (sub + row // 48) * 192 + index * 48 if turned else index * 192 + sub * 48 + row
            out[start : start + 48] = piece[row : row + 48, : out.shape[1]]


def stacked(spots, pieces, turned, columns):
    rows = sum(p.shape[0] for p in pieces)
    return pl.pallas_call(
        functools.partial(stack_kernel, spots, turned),
        in_specs=in_vmem(len(pieces)),
        out_specs=in_vmem(1)[0],
        out_shape=jax.ShapeDtypeStruct((rows, columns), bf16),
        compiler_params=pltpu.CompilerParams(**PARAMS),
        cost_estimate=pl.CostEstimate(flops=0, bytes_accessed=3 << 20, transcendentals=0),
        name="stacked",
    )(*pieces)


def prepare_kernel(device, positions, counts, targets, states, keep, give):
    cap, core = keep.shape[0], device[0] & 1
    row = lax.broadcasted_iota(i32, (8, META), 0)
    lane = lax.broadcasted_iota(i32, (8, META), 1)
    token, fields = jnp.full((8, META), -1, i32), jnp.zeros((8, META), i32)
    for s in range(cap):
        slot, target = device[0] * cap + s, targets[s]
        values = (
            slot & 255,
            slot >> 8,
            jnp.where(s < counts[0], 1, 0),
            target & 255,
            (target >> 8) & 255,
            target >> 16,
        )
        token = jnp.where(row == s, positions[s], token)
        for index, value in enumerate(values):
            fields = jnp.where((row == s) & (lane == index), value, fields)
    pick = (token == lane).astype(bf16)
    meta = fields.astype(f32).astype(bf16)
    rows = jnp.dot(pick, states[...], preferred_element_type=f32)
    mine = jnp.where(core == 0, rows[:, :SIDE], rows[:, SIDE:]).astype(bf16)
    theirs = jnp.where(core == 0, rows[:, SIDE:], rows[:, :SIDE]).astype(bf16)
    for out, value in ((keep, mine), (give, theirs)):
        out[:, :SIDE] = value[:cap]
        out[:, SIDE:] = meta[:cap]


def prepare_call(device, positions, counts, targets, states):
    shape = jax.ShapeDtypeStruct((positions.shape[0], SIDE + META), bf16)
    return pl.pallas_call(
        prepare_kernel,
        in_specs=[pl.BlockSpec(memory_space=pltpu.SMEM)] * 4 + in_vmem(1),
        out_specs=in_vmem(2),
        out_shape=[shape, shape],
        compiler_params=pltpu.CompilerParams(**PARAMS),
        name="prepare",
    )(device, positions, counts, targets, states)


def ranks_kernel(device, meta, place, slots):
    core = device[0] & 1
    pick = (
        lax.broadcasted_iota(i32, (8, META), 0) == lax.broadcasted_iota(i32, (8, META), 1)
    ).astype(bf16)
    rows = rows_dot(pick, meta[...])
    column = meta[:, :3].astype(f32)
    key, live = column[:, 0:1] + 256.0 * column[:, 1:2], column[:, 2:3]
    row_key, row_live = rows[0:1] + 256.0 * rows[1:2], rows[2:3]
    lane = lax.broadcasted_iota(i32, (1, LIVE), 1) + core * HALF
    own_rank = jnp.where(lane >= LIVE, lane - LIVE, lane).astype(f32)
    alive = row_live > 0.5
    rank = jnp.sum(jnp.where(key < row_key, live, 0.0), axis=0, keepdims=True)
    rank = jnp.where(alive, rank, -1.0).astype(i32)
    turn = rank + (1 - core) * HALF
    turn = jnp.where(turn >= LIVE, turn - LIVE, turn)
    turn = jnp.where(alive, turn, -1)
    label = [rows[k : k + 1].astype(i32) for k in (3, 4, 5)]
    label = label[0] + 256 * label[1] + 65536 * label[2] - device[0] * VOCAB_ROWS
    place[...] = jnp.concatenate([rank, turn, label] + [jnp.zeros_like(rank)] * 5, axis=0)
    down = jnp.sum(jnp.where(row_key < key, row_live, 0.0), axis=1, keepdims=True)
    hit = (down == own_rank) & (live > 0.5)
    slots[...] = jnp.sum(jnp.where(hit, key, 0.0), axis=0, keepdims=True).astype(i32)


def ranks_call(device, rows):
    count = rows.shape[0]
    whole = lambda shape: pl.BlockSpec(shape, lambda i: (0, 0))
    return pl.pallas_call(
        ranks_kernel,
        grid=(1,),
        in_specs=[
            pl.BlockSpec(memory_space=pltpu.SMEM),
            pl.BlockSpec((count, META), lambda i: (0, SIDE // META)),
        ],
        out_specs=[whole((8, count)), whole((1, LIVE))],
        out_shape=[jax.ShapeDtypeStruct((8, count), i32), jax.ShapeDtypeStruct((1, LIVE), i32)],
        compiler_params=pltpu.CompilerParams(**PARAMS),
        cost_estimate=pl.CostEstimate(flops=1 << 22, bytes_accessed=1 << 18, transcendentals=0),
        name="ranks",
    )(device, rows)


def near_kernel(device, table, rows, logits):
    start = pl.multiple_of((device[0] & 1) * SIDE, SIDE)
    logits[...] = rows_dot(table[:, pl.ds(start, SIDE)], rows[:, :SIDE])


def far_kernel(device, table, rows, partial, place, logits, stats):
    start = pl.multiple_of((1 - (device[0] & 1)) * SIDE, SIDE)
    values = partial[...] + rows_dot(table[:, pl.ds(start, SIDE)], rows[:, :SIDE])
    logits[...] = values
    top = jnp.max(values, axis=0, keepdims=True)
    total = jnp.sum(jnp.exp(values - top), axis=0, keepdims=True)
    found = jnp.concatenate([top, total], axis=0)
    stats[...] = rows_dot(found, one_hot(place[0:1]).astype(f32), precision=EXACT)


def logits_call(device, table, rows, extra=()):
    vocab, count = table.shape[0], rows.shape[0]
    shapes = [jax.ShapeDtypeStruct((vocab, count), f32), jax.ShapeDtypeStruct((2, LIVE), f32)]
    shapes = shapes if extra else shapes[:1]
    return pl.pallas_call(
        far_kernel if extra else near_kernel,
        in_specs=[pl.BlockSpec(memory_space=pltpu.SMEM)] + in_vmem(2 + len(extra)),
        out_specs=in_vmem(len(shapes)),
        out_shape=shapes,
        compiler_params=pltpu.CompilerParams(**PARAMS),
        cost_estimate=pl.CostEstimate(
            flops=vocab * count * WIDTH, bytes_accessed=4 << 20, transcendentals=vocab * count
        ),
        name="logits",
    )(device, table, rows, *extra)


def chunk_dot(device, core, g, value, table):
    parts = []
    for j in range(4):
        y_to, z_to = dp_place(device, core, EMIT[g], j)
        start = pl.multiple_of(y_to * CHUNK + z_to * 256, 256)
        parts.append(jnp.dot(value, table[:, pl.ds(start, 256)], preferred_element_type=f32))
    return jnp.concatenate(parts, axis=1)


def dlogits_kernel(device, lg, place, stats, table, grads, keep, *outs):
    rank, turn, label = place[0:1], place[1:2], place[2:3]
    where = lax.dot_general(
        stats[...],
        one_hot(rank).astype(f32),
        (((1,), (0,)), ((), ())),
        preferred_element_type=f32,
        precision=EXACT,
    )
    alive = rank >= 0
    top = jnp.where(alive, where[0:1], 0.0)
    total = jnp.where(alive, where[1:2], 1.0)
    values = lg[...]
    soft = jnp.exp(values - top) / total
    hit = lax.broadcasted_iota(i32, values.shape, 0) == label
    grad = jnp.where(alive, soft - jnp.where(hit, 1.0, 0.0), 0.0).astype(bf16)
    grads[...] = grad
    packed = rows_dot(one_hot(turn).astype(bf16), grad).astype(bf16)
    keep[...] = packed[HALF:]
    theirs = packed[:HALF]
    for g, out in enumerate(outs):
        out[...] = chunk_dot(device, 1 - (device[0] & 1), g, theirs, table).astype(bf16)


def dlogits_call(device, logits, place, stats, table):
    vocab = table.shape[0]
    out_shapes = [jax.ShapeDtypeStruct((vocab, SLOTS), bf16)]
    out_shapes += [jax.ShapeDtypeStruct((HALF, vocab), bf16)]
    out_shapes += [jax.ShapeDtypeStruct((HALF, CHUNK), bf16)] * 4
    return pl.pallas_call(
        dlogits_kernel,
        in_specs=[pl.BlockSpec(memory_space=pltpu.SMEM)] + in_vmem(4),
        out_specs=in_vmem(6),
        out_shape=out_shapes,
        compiler_params=pltpu.CompilerParams(**PARAMS),
        cost_estimate=pl.CostEstimate(
            flops=2 * vocab * HALF * WIDTH, bytes_accessed=4 << 20, transcendentals=vocab * SLOTS
        ),
        name="dlogits",
    )(device, logits, place, stats, table)


def own_kernel(device, packed, table, *outs):
    for g, out in enumerate(outs):
        out[...] = chunk_dot(device, device[0] & 1, g, packed[...], table)


def own_call(device, packed, table):
    vocab = table.shape[0]
    return pl.pallas_call(
        own_kernel,
        in_specs=[pl.BlockSpec(memory_space=pltpu.SMEM)] + in_vmem(2),
        out_specs=in_vmem(4),
        out_shape=[jax.ShapeDtypeStruct((HALF, CHUNK), f32)] * 4,
        compiler_params=pltpu.CompilerParams(**PARAMS),
        cost_estimate=pl.CostEstimate(
            flops=2 * vocab * HALF * WIDTH, bytes_accessed=4 << 20, transcendentals=0
        ),
        name="own_width",
    )(device, packed, table)


def gelu_kernel(device, pre, active, slope):
    values = pre[...].astype(f32)
    active[...] = (0.5 * values * (1.0 + lax.erf(values * half_root))).astype(bf16)

    @pl.when(pl.program_id(0) == device[0] >> 6)
    def _():
        start = pl.multiple_of(((device[0] >> 4) & 3) * 48, 16)
        slope[...] = gelu_slope(pre[pl.ds(start, 48), :].astype(f32))


def gelu_call(device, pre):
    rows, units = pre.shape
    block = pl.BlockSpec((rows // 4, units), lambda i: (i, 0))
    return pl.pallas_call(
        gelu_kernel,
        grid=(4,),
        in_specs=[pl.BlockSpec(memory_space=pltpu.SMEM), block],
        out_specs=[block, pl.BlockSpec((48, units), lambda i: (0, 0))],
        out_shape=[
            jax.ShapeDtypeStruct((rows, units), bf16),
            jax.ShapeDtypeStruct((48, units), f32),
        ],
        compiler_params=pltpu.CompilerParams(**PARAMS),
        cost_estimate=pl.CostEstimate(
            flops=rows * units * 30, bytes_accessed=rows * units * 4, transcendentals=rows * units
        ),
        name="gelu",
    )(device, pre)


def hidden_kernel(device, own, other, slots, down, rows, *outs):
    place = lax.broadcasted_iota(i32, (SLOTS, LIVE), 0) == slots[...]
    compact = jnp.concatenate([own[...], other[...]], axis=0)
    rows[...] = jnp.dot(place.astype(bf16), compact, preferred_element_type=f32).astype(bf16)
    for k, out in zip(EMIT, outs):
        parts = []
        for j in range(4):
            y_to, z_to = dp_place(device, device[0] & 1, k, j)
            start = y_to * 192 + z_to * 48
            parts.append(rows[pl.ds(pl.multiple_of(start, 16), 48), :])
        out[...] = rows_dot(jnp.concatenate(parts, axis=0), down[...]).astype(out.dtype)


def hidden_call(device, own, other, slots, down):
    shapes = [jax.ShapeDtypeStruct((SLOTS, own.shape[1]), bf16)]
    shapes += [jax.ShapeDtypeStruct((192, down.shape[0]), f32 if k == 0 else bf16) for k in EMIT]
    return pl.pallas_call(
        hidden_kernel,
        in_specs=[pl.BlockSpec(memory_space=pltpu.SMEM)] + in_vmem(4),
        out_specs=in_vmem(len(shapes)),
        out_shape=shapes,
        compiler_params=pltpu.CompilerParams(**PARAMS),
        cost_estimate=pl.CostEstimate(flops=10**9, bytes_accessed=4 << 20, transcendentals=0),
        name="hidden",
    )(device, own, other, slots, down)


def table_grad_kernel(device, grads, near, far, out, kept, sems):
    core = device[0] & 1
    copies = []
    for j in range(4):
        rows, half = (near, core) if j < 2 else (far, 1 - core)
        here = slice(j % 2 * CHUNK, (j % 2 + 1) * CHUNK)
        kept[j] = jnp.dot(grads[...], rows[:, here], preferred_element_type=f32).astype(bf16)
        start = pl.multiple_of(half * SIDE + j % 2 * CHUNK, CHUNK)
        copies.append(
            pltpu.make_async_copy(kept.at[j], out.at[:, pl.ds(start, CHUNK)], sems.at[j])
        )
        copies[-1].start()
    for copy in copies:
        copy.wait()


def table_grad_call(device, grads, near, far):
    vocab, count = grads.shape
    return pl.pallas_call(
        table_grad_kernel,
        in_specs=[pl.BlockSpec(memory_space=pltpu.SMEM)] + in_vmem(3),
        out_specs=anywhere(1)[0],
        out_shape=jax.ShapeDtypeStruct((vocab, WIDTH), bf16),
        scratch_shapes=[pltpu.VMEM((4, vocab, CHUNK), bf16), pltpu.SemaphoreType.DMA((4,))],
        compiler_params=pltpu.CompilerParams(**PARAMS),
        cost_estimate=pl.CostEstimate(
            flops=2 * vocab * count * WIDTH, bytes_accessed=4 << 20, transcendentals=0
        ),
        name="table_grad",
    )(device, grads, near, far)


def local(states, positions, counts, targets, table, h_pre, w_down):
    dp, mp = lax.axis_index("dp"), lax.axis_index("mp")
    device = dp * 16 + mp
    where = device.astype(i32)[None]

    keep, give = prepare_call(where, positions, counts, targets, states)
    got = send(give, across)
    even = mp % 2 == 0
    rows = jnp.stack([jnp.where(even, keep, got), jnp.where(even, got, keep)])
    spread = jnp.broadcast_to(rows[None], (NZ, *rows.shape))
    z_groups = [
        [spot(x, y, z, c) for z in range(NZ)]
        for x in range(NX)
        for y in range(NY)
        for c in range(NC)
    ]
    xy_groups = [
        [spot(x, y, z, c) for x in range(NX) for y in range(NY)]
        for z in range(NZ)
        for c in range(NC)
    ]
    block = lax.all_to_all(spread, BOTH, 0, 0, axis_index_groups=z_groups, tiled=True)
    block = block.reshape(-1, SIDE + META)

    wide, tall = by_core(along_y, along_x), by_core(along_x, along_y)
    block = jnp.concatenate([block] + [send(block, wide[k]) for k in (1, 2, 3)], axis=0)
    low, high = block[: 2 * 48], block[2 * 48 :]
    one_low = send(low, tall[1])
    three_high = send(high, tall[3])
    one_high = send(high, tall[1])
    three_low = send(low, tall[3])
    two_low = send(one_low, tall[3])
    two_high = send(three_high, tall[1])
    spots = ((0, 0), (1, 0), (3, 2), (1, 2), (3, 0), (2, 0), (2, 2))
    pieces = [block, one_low, three_high, one_high, three_low, two_low, two_high]
    crossing = [send(p, across) for p in pieces]
    near = stacked(spots, pieces, False, SIDE + META)
    place, slot_of = ranks_call(where, near)
    (logits,) = logits_call(where, table, near)
    far = stacked(spots, crossing, True, SIDE)
    logits, stats = logits_call(where, table, far, (logits, place))

    def spread_merge(value, groups):
        count = len(groups[0])
        sent = jnp.broadcast_to(value[None], (count, *value.shape))
        got = lax.all_to_all(sent, BOTH, 0, 0, axis_index_groups=groups, tiled=True)
        return merged([got[:, 0], got[:, 1]])

    def merged(parts):
        tops, totals = parts
        largest = jnp.max(tops, axis=0)
        return jnp.stack([largest, jnp.sum(totals * jnp.exp(tops - largest), axis=0)])

    pair = jnp.stack([stats, send(stats, across)])
    stats = merged([pair[:, 0], pair[:, 1]])
    stats = spread_merge(stats, xy_groups)
    stats = spread_merge(stats, z_groups)

    grads, keep, *away = dlogits_call(
        where, logits, place, stats, table
    )
    keep, h_pre = lax.optimization_barrier((keep, h_pre))
    activated, slope = gelu_call(where, h_pre)
    came = [send(a, across) for a in away]
    mine = own_call(where, keep, table)
    sums = [m + c.astype(f32) for m, c in zip(mine, came)]

    def scattered(chunks, along):
        return chunks[0], [send(chunks[k].astype(bf16), along[k]) for k in (1, 3, 2)]

    def total(own, parts):
        return sum([p.astype(f32) for p in parts], own)

    def relayed(own, one, three, two):
        half = own.shape[0] // 2
        low, high = slice(0, half), slice(half, None)
        via_one = send(two[low].astype(bf16), first[1])
        via_three = send(two[high].astype(bf16), first[3])
        plain_one = send(one[low].astype(bf16), first[1])
        plain_three = send(three[high].astype(bf16), first[3])
        joined_three = (three[low].astype(f32) + via_one.astype(f32)).astype(bf16)
        joined_one = (one[high].astype(f32) + via_three.astype(f32)).astype(bf16)
        joined_three = send(joined_three, first[3])
        joined_one = send(joined_one, first[1])
        return (
            total(own[low], [plain_one, joined_three]),
            total(own[high], [joined_one, plain_three]),
        )

    chunks = {k: sums[g] for g, k in enumerate(EMIT)}
    halves = relayed(chunks[0], chunks[1], chunks[3], chunks[2])
    quarter = CHUNK // 4
    chunks = {
        j: jnp.concatenate([h[:, j * quarter : (j + 1) * quarter] for h in halves], axis=0)
        for j in range(4)
    }
    own, parts = scattered(chunks, second)
    width = total(own, parts)
    narrow = width.astype(bf16)
    width = total(width, [send(narrow, along_x[k]) for k in (1, 3, 2)])
    width = width + send(width, z_pair)
    width = width.astype(bf16)
    grad_rows, *chunks = hidden_call(where, width, send(width, across), slot_of, w_down)
    chunks = dict(zip(EMIT, chunks))
    block_rows = SLOTS // 16
    low, high = relayed(chunks[0], chunks[1], chunks[3], chunks[2])
    chunks = {j: (low, high)[j // 2][j % 2 * block_rows :][:block_rows] for j in range(4)}
    own, parts = scattered(chunks, second)
    hidden_grad = total(own, parts) * slope

    table_grad = table_grad_call(where, grads, near, far)
    w_down_grad = jnp.einsum("rf,rd->fd", activated, grad_rows, preferred_element_type=f32)
    return (table_grad, w_down_grad, hidden_grad)


def solution(mesh):
    in_specs = (
        P(BOTH, None),
        P(BOTH),
        P(BOTH),
        P(BOTH),
        P(BOTH, None),
        P(None, "mp"),
        P("mp", "dp"),
    )
    out_specs = (P(BOTH, None), P("mp", "dp"), P("dp", "mp"))
    return jax.shard_map(local, mesh=mesh, in_specs=in_specs, out_specs=out_specs, check_vma=False)
```

```python
import functools

import jax
import jax.numpy as jnp
import numpy as np
from jax import lax
from jax.experimental import pallas as pl
from jax.experimental.pallas import tpu as pltpu
from jax.sharding import PartitionSpec as P

half_root = 0.7071067811865476
density_scale = 0.3989422804014327
f32, bf16, i32 = jnp.float32, jnp.bfloat16, jnp.int32
NX, NY, NZ, NC = 4, 4, 8, 2
BOTH = ("dp", "mp")
SLOTS, LIVE, WIDTH, META, VOCAB_ROWS = 768, 384, 4096, 128, 496
HALF, CHUNK, SIDE = LIVE // 2, WIDTH // 4, WIDTH // 2
EMIT = (2, 1, 3, 0)
ORDER = (0, 1, 3, 2)
PARAMS = dict(vmem_limit_bytes=16 * 2**20)
EXACT = lax.Precision.HIGHEST


def spot(x, y, z, c):
    return (y * 4 + z // 2) * 16 + (z % 2) * 8 + x * 2 + c


PLACES = [(x, y, z, c) for x in range(NX) for y in range(NY) for z in range(NZ) for c in range(NC)]


def send(value, perm):
    return lax.ppermute(value, BOTH, perm)


def crossed(mx=0, my=0, mz=0, mc=0):
    return [(spot(x, y, z, c), spot(x ^ mx, y ^ my, z ^ mz, c ^ mc)) for x, y, z, c in PLACES]


across, z_pair = crossed(mc=1), crossed(mz=1)
along_x = {k: crossed(mx=k) for k in (1, 3, 2)}
along_y = {k: crossed(my=k) for k in (1, 3, 2)}
along_z = {k: crossed(mz=2 * k) for k in (1, 3, 2)}


def by_core(zero, one):
    return {k: [p for p in zero[k] if p[0] % 2 == 0] + [p for p in one[k] if p[0] % 2] for k in (1, 3, 2)}


first, second = by_core(along_y, along_z), by_core(along_z, along_y)


def dp_place(device, core, k, j):
    y_at, z_hi = device[0] >> 6, (device[0] >> 4) & 3
    return y_at ^ jnp.where(core == 0, k, j), z_hi ^ jnp.where(core == 0, j, k)


def rows_dot(a, b, **kw):
    return lax.dot_general(a, b, (((1,), (1,)), ((), ())), preferred_element_type=f32, **kw)


def gelu_slope(inputs):
    return (
        0.5 * (1.0 + lax.erf(inputs * half_root))
        + inputs * jnp.exp(-0.5 * inputs * inputs) * density_scale
    )


def digits(values):
    return [values % 256, (values // 256) % 256, values // 65536]


def one_hot(rank):
    return lax.broadcasted_iota(i32, (LIVE, rank.shape[1]), 0) == rank


def in_vmem(count):
    return [pl.BlockSpec(memory_space=pltpu.VMEM)] * count


def anywhere(count):
    return [pl.BlockSpec(memory_space=pl.ANY)] * count


def stack_kernel(spots, turned, *refs):
    *pieces, out = refs
    for (index, sub), piece in zip(spots, pieces):
        for row in range(0, piece.shape[0], 48):
            start = index * 192 + sub * 48 + row
            if turned:
                start = ORDER.index(sub + row // 48) * 192 + ORDER[index] * 48
            out[start : start + 48] = piece[row : row + 48, : out.shape[1]]


def stacked(spots, pieces, turned, columns):
    rows = sum(p.shape[0] for p in pieces)
    return pl.pallas_call(
        functools.partial(stack_kernel, spots, turned),
        in_specs=in_vmem(len(pieces)),
        out_specs=in_vmem(1)[0],
        out_shape=jax.ShapeDtypeStruct((rows, columns), bf16),
        compiler_params=pltpu.CompilerParams(**PARAMS),
        cost_estimate=pl.CostEstimate(flops=0, bytes_accessed=3 << 20, transcendentals=0),
        name="stacked",
    )(*pieces)


def prepare_kernel(device, *refs):
    sources, (keep, give), kept, sems = refs[:4], refs[4:6], refs[6:10], refs[10]
    copies = [pltpu.make_async_copy(s, k, sems.at[i]) for i, (s, k) in enumerate(zip(sources, kept))]
    for copy in copies:
        copy.start()
    for copy in copies:
        copy.wait()
    positions, counts, targets, states = kept
    cap, core = keep.shape[0], device[0] & 1
    row = lax.broadcasted_iota(i32, (8, META), 0)
    lane = lax.broadcasted_iota(i32, (8, META), 1)
    token, fields = jnp.full((8, META), -1, i32), jnp.zeros((8, META), i32)
    for s in range(cap):
        slot, target = device[0] * cap + s, targets[s]
        values = (
            slot & 255,
            slot >> 8,
            jnp.where(s < counts[0], 1, 0),
            target & 255,
            (target >> 8) & 255,
            target >> 16,
        )
        token = jnp.where(row == s, positions[s], token)
        for index, value in enumerate(values):
            fields = jnp.where((row == s) & (lane == index), value, fields)
    pick = (token == lane).astype(bf16)
    meta = fields.astype(f32).astype(bf16)
    rows = jnp.dot(pick, states[...], preferred_element_type=f32)
    mine = jnp.where(core == 0, rows[:, :SIDE], rows[:, SIDE:]).astype(bf16)
    theirs = jnp.where(core == 0, rows[:, SIDE:], rows[:, :SIDE]).astype(bf16)
    for out, value in ((keep, mine), (give, theirs)):
        out[:, :SIDE] = value[:cap]
        out[:, SIDE:] = meta[:cap]


def prepare_call(device, positions, counts, targets, states):
    shape = jax.ShapeDtypeStruct((positions.shape[0], SIDE + META), bf16)
    return pl.pallas_call(
        prepare_kernel,
        in_specs=[pl.BlockSpec(memory_space=pltpu.SMEM)] + anywhere(4),
        out_specs=in_vmem(2),
        out_shape=[shape, shape],
        scratch_shapes=[pltpu.SMEM(a.shape, i32) for a in (positions, counts, targets)]
        + [pltpu.VMEM(states.shape, bf16), pltpu.SemaphoreType.DMA((4,))],
        compiler_params=pltpu.CompilerParams(vmem_limit_bytes=60 * 2**20),
        name="prepare",
    )(device, positions, counts, targets, states)


def ranks_kernel(device, early, late, place, slots):
    core = device[0] & 1
    meta = jnp.concatenate([early[...], late[...]], axis=0)
    pick = (
        lax.broadcasted_iota(i32, (8, META), 0) == lax.broadcasted_iota(i32, (8, META), 1)
    ).astype(bf16)
    rows = rows_dot(pick, meta)
    column = meta[:, :3].astype(f32)
    key, live = column[:, 0:1] + 256.0 * column[:, 1:2], column[:, 2:3]
    row_key, row_live = rows[0:1] + 256.0 * rows[1:2], rows[2:3]
    lane = lax.broadcasted_iota(i32, (1, LIVE), 1) + core * HALF
    own_rank = jnp.where(lane >= LIVE, lane - LIVE, lane).astype(f32)
    alive = row_live > 0.5
    rank = jnp.sum(jnp.where(key < row_key, live, 0.0), axis=0, keepdims=True)
    rank = jnp.where(alive, rank, -1.0).astype(i32)
    turn = rank + (1 - core) * HALF
    turn = jnp.where(turn >= LIVE, turn - LIVE, turn)
    turn = jnp.where(alive, turn, -1)
    label = [rows[k : k + 1].astype(i32) for k in (3, 4, 5)]
    label = label[0] + 256 * label[1] + 65536 * label[2] - device[0] * VOCAB_ROWS
    place[...] = jnp.concatenate([rank, turn, label] + [jnp.zeros_like(rank)] * 5, axis=0)
    down = jnp.sum(jnp.where(row_key < key, row_live, 0.0), axis=1, keepdims=True)
    hit = (down == own_rank) & (live > 0.5)
    slots[...] = jnp.sum(jnp.where(hit, key, 0.0), axis=0, keepdims=True).astype(i32)


def ranks_call(device, early, late):
    count = early.shape[0] + late.shape[0]
    whole = lambda shape: pl.BlockSpec(shape, lambda i: (0, 0))
    return pl.pallas_call(
        ranks_kernel,
        grid=(1,),
        in_specs=[
            pl.BlockSpec(memory_space=pltpu.SMEM),
            pl.BlockSpec((early.shape[0], META), lambda i: (0, SIDE // META)),
            pl.BlockSpec((late.shape[0], META), lambda i: (0, SIDE // META)),
        ],
        out_specs=[whole((8, count)), whole((1, LIVE))],
        out_shape=[jax.ShapeDtypeStruct((8, count), i32), jax.ShapeDtypeStruct((1, LIVE), i32)],
        compiler_params=pltpu.CompilerParams(**PARAMS),
        cost_estimate=pl.CostEstimate(flops=1 << 22, bytes_accessed=1 << 18, transcendentals=0),
        name="ranks",
    )(device, early, late)


def near_kernel(device, table, rows, logits):
    start = pl.multiple_of((device[0] & 1) * SIDE, SIDE)
    logits[...] = rows_dot(table[:, pl.ds(start, SIDE)], rows[:, :SIDE])


def far_kernel(device, table, rows, early, late, place, logits, stats):
    start = pl.multiple_of((1 - (device[0] & 1)) * SIDE, SIDE)
    partial = jnp.concatenate([early[...], late[...]], axis=1)
    values = partial + rows_dot(table[:, pl.ds(start, SIDE)], rows[:, :SIDE])
    logits[...] = values
    top = jnp.max(values, axis=0, keepdims=True)
    total = jnp.sum(jnp.exp(values - top), axis=0, keepdims=True)
    found = jnp.concatenate([top, total], axis=0)
    stats[...] = rows_dot(found, one_hot(place[0:1]).astype(f32), precision=EXACT)


def logits_call(device, table, rows, extra=()):
    vocab, count = table.shape[0], rows.shape[0]
    shapes = [jax.ShapeDtypeStruct((vocab, count), f32), jax.ShapeDtypeStruct((2, LIVE), f32)]
    shapes = shapes if extra else shapes[:1]
    return pl.pallas_call(
        far_kernel if extra else near_kernel,
        in_specs=[pl.BlockSpec(memory_space=pltpu.SMEM)] + in_vmem(2 + len(extra)),
        out_specs=in_vmem(len(shapes)),
        out_shape=shapes,
        compiler_params=pltpu.CompilerParams(**PARAMS),
        cost_estimate=pl.CostEstimate(
            flops=vocab * count * WIDTH, bytes_accessed=4 << 20, transcendentals=vocab * count
        ),
        name="logits",
    )(device, table, rows, *extra)


def chunk_dot(device, core, g, value, table):
    parts = []
    for j in range(4):
        y_to, z_to = dp_place(device, core, EMIT[g], j)
        start = pl.multiple_of(y_to * CHUNK + z_to * 256, 256)
        parts.append(jnp.dot(value, table[:, pl.ds(start, 256)], preferred_element_type=f32))
    return jnp.concatenate(parts, axis=1)


def dlogits_kernel(device, lg, place, stats, table, grads, keep, *outs):
    rank, turn, label = place[0:1], place[1:2], place[2:3]
    where = lax.dot_general(
        stats[...],
        one_hot(rank).astype(f32),
        (((1,), (0,)), ((), ())),
        preferred_element_type=f32,
        precision=EXACT,
    )
    alive = rank >= 0
    top = jnp.where(alive, where[0:1], 0.0)
    total = jnp.where(alive, where[1:2], 1.0)
    values = lg[...]
    soft = jnp.exp(values - top) / total
    hit = lax.broadcasted_iota(i32, values.shape, 0) == label
    grad = jnp.where(alive, soft - jnp.where(hit, 1.0, 0.0), 0.0).astype(bf16)
    grads[...] = grad
    packed = rows_dot(one_hot(turn).astype(bf16), grad).astype(bf16)
    keep[...] = packed[HALF:]
    theirs = packed[:HALF]
    for g, out in enumerate(outs):
        out[...] = chunk_dot(device, 1 - (device[0] & 1), g, theirs, table).astype(bf16)


def dlogits_call(device, logits, place, stats, table):
    vocab = table.shape[0]
    out_shapes = [jax.ShapeDtypeStruct((vocab, SLOTS), bf16)]
    out_shapes += [jax.ShapeDtypeStruct((HALF, vocab), bf16)]
    out_shapes += [jax.ShapeDtypeStruct((HALF, CHUNK), bf16)] * 4
    return pl.pallas_call(
        dlogits_kernel,
        in_specs=[pl.BlockSpec(memory_space=pltpu.SMEM)] + in_vmem(4),
        out_specs=in_vmem(6),
        out_shape=out_shapes,
        compiler_params=pltpu.CompilerParams(**PARAMS),
        cost_estimate=pl.CostEstimate(
            flops=2 * vocab * HALF * WIDTH, bytes_accessed=4 << 20, transcendentals=vocab * SLOTS
        ),
        name="dlogits",
    )(device, logits, place, stats, table)


def own_kernel(device, packed, table, *outs):
    for g, out in enumerate(outs):
        out[...] = chunk_dot(device, device[0] & 1, g, packed[...], table)


def own_call(device, packed, table):
    vocab = table.shape[0]
    return pl.pallas_call(
        own_kernel,
        in_specs=[pl.BlockSpec(memory_space=pltpu.SMEM)] + in_vmem(2),
        out_specs=in_vmem(4),
        out_shape=[jax.ShapeDtypeStruct((HALF, CHUNK), f32)] * 4,
        compiler_params=pltpu.CompilerParams(**PARAMS),
        cost_estimate=pl.CostEstimate(
            flops=2 * vocab * HALF * WIDTH, bytes_accessed=4 << 20, transcendentals=0
        ),
        name="own_width",
    )(device, packed, table)


def gelu_kernel(device, pre, active, slope):
    values = pre[...].astype(f32)
    active[...] = (0.5 * values * (1.0 + lax.erf(values * half_root))).astype(bf16)

    @pl.when(pl.program_id(0) == device[0] >> 6)
    def _():
        start = pl.multiple_of(((device[0] >> 4) & 3) * 48, 16)
        slope[...] = gelu_slope(pre[pl.ds(start, 48), :].astype(f32))


def gelu_call(device, pre):
    rows, units = pre.shape
    block = pl.BlockSpec((rows // 4, units), lambda i: (i, 0))
    return pl.pallas_call(
        gelu_kernel,
        grid=(4,),
        in_specs=[pl.BlockSpec(memory_space=pltpu.SMEM), block],
        out_specs=[block, pl.BlockSpec((48, units), lambda i: (0, 0))],
        out_shape=[
            jax.ShapeDtypeStruct((rows, units), bf16),
            jax.ShapeDtypeStruct((48, units), f32),
        ],
        compiler_params=pltpu.CompilerParams(**PARAMS),
        cost_estimate=pl.CostEstimate(
            flops=rows * units * 30, bytes_accessed=rows * units * 4, transcendentals=rows * units
        ),
        name="gelu",
    )(device, pre)


def hidden_kernel(device, own, other, slots, down, rows, *outs):
    place = lax.broadcasted_iota(i32, (SLOTS, LIVE), 0) == slots[...]
    compact = jnp.concatenate([own[...], other[...]], axis=0)
    rows[...] = jnp.dot(place.astype(bf16), compact, preferred_element_type=f32).astype(bf16)
    for k, out in zip(EMIT, outs):
        parts = []
        for j in range(4):
            y_to, z_to = dp_place(device, device[0] & 1, k, j)
            start = y_to * 192 + z_to * 48
            parts.append(rows[pl.ds(pl.multiple_of(start, 16), 48), :])
        out[...] = rows_dot(jnp.concatenate(parts, axis=0), down[...]).astype(out.dtype)


def hidden_call(device, own, other, slots, down):
    shapes = [jax.ShapeDtypeStruct((SLOTS, own.shape[1]), bf16)]
    shapes += [jax.ShapeDtypeStruct((192, down.shape[0]), f32 if k == 0 else bf16) for k in EMIT]
    return pl.pallas_call(
        hidden_kernel,
        in_specs=[pl.BlockSpec(memory_space=pltpu.SMEM)] + in_vmem(4),
        out_specs=in_vmem(len(shapes)),
        out_shape=shapes,
        compiler_params=pltpu.CompilerParams(**PARAMS),
        cost_estimate=pl.CostEstimate(flops=10**9, bytes_accessed=4 << 20, transcendentals=0),
        name="hidden",
    )(device, own, other, slots, down)


def table_grad_kernel(device, grads, early, late, far, out, kept, sems):
    core = device[0] & 1
    copies = []
    for j in range(4):
        half = core if j < 2 else 1 - core
        here = slice(j % 2 * CHUNK, (j % 2 + 1) * CHUNK)
        if j < 2:
            rows = jnp.concatenate([early[:, here], late[:, here]], axis=0)
        else:
            rows = far[:, here]
        kept[j] = jnp.dot(grads[...], rows, preferred_element_type=f32).astype(bf16)
        start = pl.multiple_of(half * SIDE + j % 2 * CHUNK, CHUNK)
        copies.append(
            pltpu.make_async_copy(kept.at[j], out.at[:, pl.ds(start, CHUNK)], sems.at[j])
        )
        copies[-1].start()
    for copy in copies:
        copy.wait()


def table_grad_call(device, grads, early, late, far):
    vocab, count = grads.shape
    return pl.pallas_call(
        table_grad_kernel,
        in_specs=[pl.BlockSpec(memory_space=pltpu.SMEM)] + in_vmem(4),
        out_specs=anywhere(1)[0],
        out_shape=jax.ShapeDtypeStruct((vocab, WIDTH), bf16),
        scratch_shapes=[pltpu.VMEM((4, vocab, CHUNK), bf16), pltpu.SemaphoreType.DMA((4,))],
        compiler_params=pltpu.CompilerParams(**PARAMS),
        cost_estimate=pl.CostEstimate(
            flops=2 * vocab * count * WIDTH, bytes_accessed=4 << 20, transcendentals=0
        ),
        name="table_grad",
    )(device, grads, early, late, far)


def local(states, positions, counts, targets, table, h_pre, w_down):
    dp, mp = lax.axis_index("dp"), lax.axis_index("mp")
    device = dp * 16 + mp
    where = device.astype(i32)[None]

    keep, give = prepare_call(where, positions, counts, targets, states)
    got = send(give, across)
    even = mp % 2 == 0
    rows = jnp.stack([jnp.where(even, keep, got), jnp.where(even, got, keep)])
    spread = jnp.broadcast_to(rows[None], (NZ, *rows.shape))
    z_groups = [
        [spot(x, y, z, c) for z in range(NZ)]
        for x in range(NX)
        for y in range(NY)
        for c in range(NC)
    ]
    xy_groups = [
        [spot(x, y, z, c) for x in range(NX) for y in range(NY)]
        for z in range(NZ)
        for c in range(NC)
    ]
    block = lax.all_to_all(spread, BOTH, 0, 0, axis_index_groups=z_groups, tiled=True)
    block = block.reshape(-1, SIDE + META)

    wide, tall = by_core(along_y, along_x), by_core(along_x, along_y)
    beside = {k: send(block, wide[k]) for k in (1, 3, 2)}
    block = jnp.concatenate([block] + [beside[k] for k in (1, 2, 3)], axis=0)
    low, high = block[: 2 * 48], block[2 * 48 :]
    one_low = send(low, tall[1])
    three_high = send(high, tall[3])
    one_high = send(high, tall[1])
    three_low = send(low, tall[3])
    two_low = send(one_low, tall[3])
    two_high = send(three_high, tall[1])
    spots = ((0, 0), (1, 0), (2, 2), (1, 2), (2, 0), (3, 0), (3, 2))
    pieces = [block, one_low, three_high, one_high, three_low, two_low, two_high]
    crossing = [send(p, across) for p in pieces]
    early = stacked(spots[:5], pieces[:5], False, SIDE + META)
    late = stacked(((0, 0), (0, 2)), pieces[5:], False, SIDE + META)
    (first_part,) = logits_call(where, table, early)
    (last_part,) = logits_call(where, table, late)
    place, slot_of = ranks_call(where, early, late)
    far = stacked(spots, crossing, True, SIDE)
    logits, stats = logits_call(where, table, far, (first_part, last_part, place))

    def spread_merge(value, groups):
        count = len(groups[0])
        sent = jnp.broadcast_to(value[None], (count, *value.shape))
        got = lax.all_to_all(sent, BOTH, 0, 0, axis_index_groups=groups, tiled=True)
        return merged([got[:, 0], got[:, 1]])

    def merged(parts):
        tops, totals = parts
        largest = jnp.max(tops, axis=0)
        return jnp.stack([largest, jnp.sum(totals * jnp.exp(tops - largest), axis=0)])

    pair = jnp.stack([stats, send(stats, across)])
    stats = merged([pair[:, 0], pair[:, 1]])
    stats = spread_merge(stats, xy_groups)
    stats = spread_merge(stats, z_groups)

    grads, keep, *away = dlogits_call(
        where, logits, place, stats, table
    )
    came = [send(a, across) for a in away]
    mine = own_call(where, keep, table)
    sums = [m + c.astype(f32) for m, c in zip(mine, came)]
    sums[0], h_pre = lax.optimization_barrier((sums[0], h_pre))
    activated, slope = gelu_call(where, h_pre)

    def scattered(chunks, along):
        return chunks[0], [send(chunks[k].astype(bf16), along[k]) for k in (1, 3, 2)]

    def total(own, parts):
        return sum([p.astype(f32) for p in parts], own)

    def relayed(own, one, three, two):
        half = own.shape[0] // 2
        low, high = slice(0, half), slice(half, None)
        via_one = send(two[low].astype(bf16), first[1])
        via_three = send(two[high].astype(bf16), first[3])
        plain_one = send(one[low].astype(bf16), first[1])
        plain_three = send(three[high].astype(bf16), first[3])
        joined_three = (three[low].astype(f32) + via_one.astype(f32)).astype(bf16)
        joined_one = (one[high].astype(f32) + via_three.astype(f32)).astype(bf16)
        joined_three = send(joined_three, first[3])
        joined_one = send(joined_one, first[1])
        return (
            total(own[low], [plain_one, joined_three]),
            total(own[high], [joined_one, plain_three]),
        )

    chunks = {k: sums[g] for g, k in enumerate(EMIT)}
    halves = relayed(chunks[0], chunks[1], chunks[3], chunks[2])
    *halves, activated, slope = lax.optimization_barrier((*halves, activated, slope))
    quarter = CHUNK // 4
    chunks = {
        j: jnp.concatenate([h[:, j * quarter : (j + 1) * quarter] for h in halves], axis=0)
        for j in range(4)
    }
    own, parts = scattered(chunks, second)
    width = total(own, parts)
    narrow = width.astype(bf16)
    width = total(width, [send(narrow, along_x[k]) for k in (1, 3, 2)])
    width = width + send(width, z_pair)
    width = width.astype(bf16)
    grad_rows, *chunks = hidden_call(where, width, send(width, across), slot_of, w_down)
    chunks = dict(zip(EMIT, chunks))
    block_rows = SLOTS // 16
    low, high = relayed(chunks[0], chunks[1], chunks[3], chunks[2])
    chunks = {j: (low, high)[j // 2][j % 2 * block_rows :][:block_rows] for j in range(4)}
    own, parts = scattered(chunks, second)
    hidden_grad = total(own, parts) * slope

    table_grad = table_grad_call(where, grads, early, late, far)
    w_down_grad = jnp.einsum("rf,rd->fd", activated, grad_rows, preferred_element_type=f32)
    return (table_grad, w_down_grad, hidden_grad)


def solution(mesh):
    in_specs = (
        P(BOTH, None),
        P(BOTH),
        P(BOTH),
        P(BOTH),
        P(BOTH, None),
        P(None, "mp"),
        P("mp", "dp"),
    )
    out_specs = (P(BOTH, None), P("mp", "dp"), P("dp", "mp"))
    return jax.shard_map(local, mesh=mesh, in_specs=in_specs, out_specs=out_specs, check_vma=False)
```

```python
import functools

import jax
import jax.numpy as jnp
import numpy as np
from jax import lax
from jax.experimental import pallas as pl
from jax.experimental.pallas import tpu as pltpu
from jax.sharding import PartitionSpec as P

half_root = 0.7071067811865476
density_scale = 0.3989422804014327
f32, bf16, i32 = jnp.float32, jnp.bfloat16, jnp.int32
NX, NY, NZ, NC = 4, 4, 8, 2
BOTH = ("dp", "mp")
SLOTS, LIVE, WIDTH, META, VOCAB_ROWS = 768, 384, 4096, 128, 496
HALF, CHUNK, SIDE = LIVE // 2, WIDTH // 4, WIDTH // 2
EMIT = (2, 1, 3, 0)
ORDER = (0, 1, 3, 2)
PARAMS = dict(vmem_limit_bytes=16 * 2**20)
EXACT = lax.Precision.HIGHEST


def spot(x, y, z, c):
    return (y * 4 + z // 2) * 16 + (z % 2) * 8 + x * 2 + c


PLACES = [(x, y, z, c) for x in range(NX) for y in range(NY) for z in range(NZ) for c in range(NC)]


def send(value, perm):
    return lax.ppermute(value, BOTH, perm)


def crossed(mx=0, my=0, mz=0, mc=0):
    return [(spot(x, y, z, c), spot(x ^ mx, y ^ my, z ^ mz, c ^ mc)) for x, y, z, c in PLACES]


across, z_pair = crossed(mc=1), crossed(mz=1)
along_x = {k: crossed(mx=k) for k in (1, 3, 2)}
along_y = {k: crossed(my=k) for k in (1, 3, 2)}
along_z = {k: crossed(mz=2 * k) for k in (1, 3, 2)}


def by_core(zero, one):
    return {k: [p for p in zero[k] if p[0] % 2 == 0] + [p for p in one[k] if p[0] % 2] for k in (1, 3, 2)}


first, second = by_core(along_y, along_z), by_core(along_z, along_y)


def dp_place(device, core, k, j):
    y_at, z_hi = device[0] >> 6, (device[0] >> 4) & 3
    return y_at ^ jnp.where(core == 0, k, j), z_hi ^ jnp.where(core == 0, j, k)


def rows_dot(a, b, **kw):
    return lax.dot_general(a, b, (((1,), (1,)), ((), ())), preferred_element_type=f32, **kw)


def gelu_slope(inputs):
    return (
        0.5 * (1.0 + lax.erf(inputs * half_root))
        + inputs * jnp.exp(-0.5 * inputs * inputs) * density_scale
    )


def digits(values):
    return [values % 256, (values // 256) % 256, values // 65536]


def one_hot(rank):
    return lax.broadcasted_iota(i32, (LIVE, rank.shape[1]), 0) == rank


def in_vmem(count):
    return [pl.BlockSpec(memory_space=pltpu.VMEM)] * count


def anywhere(count):
    return [pl.BlockSpec(memory_space=pl.ANY)] * count


def stack_kernel(spots, turned, *refs):
    *pieces, out = refs
    for (index, sub), piece in zip(spots, pieces):
        for row in range(0, piece.shape[0], 48):
            start = index * 192 + sub * 48 + row
            if turned:
                start = ORDER.index(sub + row // 48) * 192 + ORDER[index] * 48
            out[start : start + 48] = piece[row : row + 48, : out.shape[1]]


def stacked(spots, pieces, turned, columns):
    rows = sum(p.shape[0] for p in pieces)
    return pl.pallas_call(
        functools.partial(stack_kernel, spots, turned),
        in_specs=in_vmem(len(pieces)),
        out_specs=in_vmem(1)[0],
        out_shape=jax.ShapeDtypeStruct((rows, columns), bf16),
        compiler_params=pltpu.CompilerParams(**PARAMS),
        cost_estimate=pl.CostEstimate(flops=0, bytes_accessed=3 << 20, transcendentals=0),
        name="stacked",
    )(*pieces)


def prepare_kernel(device, *refs):
    sources, out, kept, sems = refs[:4], refs[4], refs[5:9], refs[9]
    copies = [pltpu.make_async_copy(s, k, sems.at[i]) for i, (s, k) in enumerate(zip(sources, kept))]
    for copy in copies:
        copy.start()
    for copy in copies:
        copy.wait()
    positions, counts, targets, states = kept
    cap = out.shape[1]
    row = lax.broadcasted_iota(i32, (8, META), 0)
    lane = lax.broadcasted_iota(i32, (8, META), 1)
    token, fields = jnp.full((8, META), -1, i32), jnp.zeros((8, META), i32)
    for s in range(cap):
        slot, target = device[0] * cap + s, targets[s]
        values = (
            slot & 255,
            slot >> 8,
            jnp.where(s < counts[0], 1, 0),
            target & 255,
            (target >> 8) & 255,
            target >> 16,
        )
        token = jnp.where(row == s, positions[s], token)
        for index, value in enumerate(values):
            fields = jnp.where((row == s) & (lane == index), value, fields)
    pick = (token == lane).astype(bf16)
    meta = fields.astype(f32).astype(bf16)
    rows = jnp.dot(pick, states[...], preferred_element_type=f32)
    for half in range(2):
        out[half, :, :SIDE] = rows[:cap, half * SIDE : (half + 1) * SIDE].astype(bf16)
        out[half, :, SIDE:] = meta[:cap]


def prepare_call(device, positions, counts, targets, states):
    shape = jax.ShapeDtypeStruct((2, positions.shape[0], SIDE + META), bf16)
    return pl.pallas_call(
        prepare_kernel,
        in_specs=[pl.BlockSpec(memory_space=pltpu.SMEM)] + anywhere(4),
        out_specs=in_vmem(1)[0],
        out_shape=shape,
        scratch_shapes=[pltpu.SMEM(a.shape, i32) for a in (positions, counts, targets)]
        + [pltpu.VMEM(states.shape, bf16), pltpu.SemaphoreType.DMA((4,))],
        compiler_params=pltpu.CompilerParams(vmem_limit_bytes=60 * 2**20),
        name="prepare",
    )(device, positions, counts, targets, states)


def ranks_kernel(device, early, late, place, slots):
    core = device[0] & 1
    meta = jnp.concatenate([early[...], late[...]], axis=0)
    pick = (
        lax.broadcasted_iota(i32, (8, META), 0) == lax.broadcasted_iota(i32, (8, META), 1)
    ).astype(bf16)
    rows = rows_dot(pick, meta)
    column = meta[:, :3].astype(f32)
    key, live = column[:, 0:1] + 256.0 * column[:, 1:2], column[:, 2:3]
    row_key, row_live = rows[0:1] + 256.0 * rows[1:2], rows[2:3]
    lane = lax.broadcasted_iota(i32, (1, LIVE), 1) + core * HALF
    own_rank = jnp.where(lane >= LIVE, lane - LIVE, lane).astype(f32)
    alive = row_live > 0.5
    rank = jnp.sum(jnp.where(key < row_key, live, 0.0), axis=0, keepdims=True)
    rank = jnp.where(alive, rank, -1.0).astype(i32)
    turn = rank + (1 - core) * HALF
    turn = jnp.where(turn >= LIVE, turn - LIVE, turn)
    turn = jnp.where(alive, turn, -1)
    label = [rows[k : k + 1].astype(i32) for k in (3, 4, 5)]
    label = label[0] + 256 * label[1] + 65536 * label[2] - device[0] * VOCAB_ROWS
    place[...] = jnp.concatenate([rank, turn, label] + [jnp.zeros_like(rank)] * 5, axis=0)
    down = jnp.sum(jnp.where(row_key < key, row_live, 0.0), axis=1, keepdims=True)
    hit = (down == own_rank) & (live > 0.5)
    slots[...] = jnp.sum(jnp.where(hit, key, 0.0), axis=0, keepdims=True).astype(i32)


def ranks_call(device, early, late):
    count = early.shape[0] + late.shape[0]
    whole = lambda shape: pl.BlockSpec(shape, lambda i: (0, 0))
    return pl.pallas_call(
        ranks_kernel,
        grid=(1,),
        in_specs=[
            pl.BlockSpec(memory_space=pltpu.SMEM),
            pl.BlockSpec((early.shape[0], META), lambda i: (0, SIDE // META)),
            pl.BlockSpec((late.shape[0], META), lambda i: (0, SIDE // META)),
        ],
        out_specs=[whole((8, count)), whole((1, LIVE))],
        out_shape=[jax.ShapeDtypeStruct((8, count), i32), jax.ShapeDtypeStruct((1, LIVE), i32)],
        compiler_params=pltpu.CompilerParams(**PARAMS),
        cost_estimate=pl.CostEstimate(flops=1 << 22, bytes_accessed=1 << 18, transcendentals=0),
        name="ranks",
    )(device, early, late)


def near_kernel(device, table, rows, logits):
    start = pl.multiple_of((device[0] & 1) * SIDE, SIDE)
    logits[...] = rows_dot(table[:, pl.ds(start, SIDE)], rows[:, :SIDE])


def far_kernel(device, table, rows, early, late, place, logits, stats):
    start = pl.multiple_of((1 - (device[0] & 1)) * SIDE, SIDE)
    partial = jnp.concatenate([early[...], late[...]], axis=1)
    values = partial + rows_dot(table[:, pl.ds(start, SIDE)], rows[:, :SIDE])
    logits[...] = values
    top = jnp.max(values, axis=0, keepdims=True)
    total = jnp.sum(jnp.exp(values - top), axis=0, keepdims=True)
    found = jnp.concatenate([top, total], axis=0)
    stats[...] = rows_dot(found, one_hot(place[0:1]).astype(f32), precision=EXACT)


def logits_call(device, table, rows, extra=()):
    vocab, count = table.shape[0], rows.shape[0]
    shapes = [jax.ShapeDtypeStruct((vocab, count), f32), jax.ShapeDtypeStruct((2, LIVE), f32)]
    shapes = shapes if extra else shapes[:1]
    return pl.pallas_call(
        far_kernel if extra else near_kernel,
        in_specs=[pl.BlockSpec(memory_space=pltpu.SMEM)] + in_vmem(2 + len(extra)),
        out_specs=in_vmem(len(shapes)),
        out_shape=shapes,
        compiler_params=pltpu.CompilerParams(**PARAMS),
        cost_estimate=pl.CostEstimate(
            flops=vocab * count * WIDTH, bytes_accessed=4 << 20, transcendentals=vocab * count
        ),
        name="logits",
    )(device, table, rows, *extra)


def chunk_dot(device, core, g, value, table):
    parts = []
    for j in range(4):
        y_to, z_to = dp_place(device, core, EMIT[g], j)
        start = pl.multiple_of(y_to * CHUNK + z_to * 256, 256)
        parts.append(jnp.dot(value, table[:, pl.ds(start, 256)], preferred_element_type=f32))
    return jnp.concatenate(parts, axis=1)


def dlogits_kernel(device, lg, place, stats, table, grads, keep, *outs):
    rank, turn, label = place[0:1], place[1:2], place[2:3]
    where = lax.dot_general(
        stats[...],
        one_hot(rank).astype(f32),
        (((1,), (0,)), ((), ())),
        preferred_element_type=f32,
        precision=EXACT,
    )
    alive = rank >= 0
    top = jnp.where(alive, where[0:1], 0.0)
    total = jnp.where(alive, where[1:2], 1.0)
    values = lg[...]
    soft = jnp.exp(values - top) / total
    hit = lax.broadcasted_iota(i32, values.shape, 0) == label
    grad = jnp.where(alive, soft - jnp.where(hit, 1.0, 0.0), 0.0).astype(bf16)
    grads[...] = grad
    packed = rows_dot(one_hot(turn).astype(bf16), grad).astype(bf16)
    keep[...] = packed[HALF:]
    theirs = packed[:HALF]
    for g, out in enumerate(outs):
        out[...] = chunk_dot(device, 1 - (device[0] & 1), g, theirs, table).astype(bf16)


def dlogits_call(device, logits, place, stats, table):
    vocab = table.shape[0]
    out_shapes = [jax.ShapeDtypeStruct((vocab, SLOTS), bf16)]
    out_shapes += [jax.ShapeDtypeStruct((HALF, vocab), bf16)]
    out_shapes += [jax.ShapeDtypeStruct((HALF, CHUNK), bf16)] * 4
    return pl.pallas_call(
        dlogits_kernel,
        in_specs=[pl.BlockSpec(memory_space=pltpu.SMEM)] + in_vmem(4),
        out_specs=in_vmem(6),
        out_shape=out_shapes,
        compiler_params=pltpu.CompilerParams(**PARAMS),
        cost_estimate=pl.CostEstimate(
            flops=2 * vocab * HALF * WIDTH, bytes_accessed=4 << 20, transcendentals=vocab * SLOTS
        ),
        name="dlogits",
    )(device, logits, place, stats, table)


def own_kernel(device, packed, table, *outs):
    for g, out in enumerate(outs):
        out[...] = chunk_dot(device, device[0] & 1, g, packed[...], table)


def own_call(device, packed, table):
    vocab = table.shape[0]
    return pl.pallas_call(
        own_kernel,
        in_specs=[pl.BlockSpec(memory_space=pltpu.SMEM)] + in_vmem(2),
        out_specs=in_vmem(4),
        out_shape=[jax.ShapeDtypeStruct((HALF, CHUNK), f32)] * 4,
        compiler_params=pltpu.CompilerParams(**PARAMS),
        cost_estimate=pl.CostEstimate(
            flops=2 * vocab * HALF * WIDTH, bytes_accessed=4 << 20, transcendentals=0
        ),
        name="own_width",
    )(device, packed, table)


def gelu_kernel(device, pre, active, slope):
    values = pre[...].astype(f32)
    active[...] = (0.5 * values * (1.0 + lax.erf(values * half_root))).astype(bf16)

    @pl.when(pl.program_id(0) == device[0] >> 6)
    def _():
        start = pl.multiple_of(((device[0] >> 4) & 3) * 48, 16)
        slope[...] = gelu_slope(pre[pl.ds(start, 48), :].astype(f32))


def gelu_call(device, pre):
    rows, units = pre.shape
    block = pl.BlockSpec((rows // 4, units), lambda i: (i, 0))
    return pl.pallas_call(
        gelu_kernel,
        grid=(4,),
        in_specs=[pl.BlockSpec(memory_space=pltpu.SMEM), block],
        out_specs=[block, pl.BlockSpec((48, units), lambda i: (0, 0))],
        out_shape=[
            jax.ShapeDtypeStruct((rows, units), bf16),
            jax.ShapeDtypeStruct((48, units), f32),
        ],
        compiler_params=pltpu.CompilerParams(**PARAMS),
        cost_estimate=pl.CostEstimate(
            flops=rows * units * 30, bytes_accessed=rows * units * 4, transcendentals=rows * units
        ),
        name="gelu",
    )(device, pre)


def hidden_kernel(device, own, other, slots, down, rows, *outs):
    place = lax.broadcasted_iota(i32, (SLOTS, LIVE), 0) == slots[...]
    compact = jnp.concatenate([own[...], other[...]], axis=0)
    rows[...] = jnp.dot(place.astype(bf16), compact, preferred_element_type=f32).astype(bf16)
    for k, out in zip(EMIT, outs):
        parts = []
        for j in range(4):
            y_to, z_to = dp_place(device, device[0] & 1, k, j)
            start = y_to * 192 + z_to * 48
            parts.append(rows[pl.ds(pl.multiple_of(start, 16), 48), :])
        out[...] = rows_dot(jnp.concatenate(parts, axis=0), down[...]).astype(out.dtype)


def hidden_call(device, own, other, slots, down):
    shapes = [jax.ShapeDtypeStruct((SLOTS, own.shape[1]), bf16)]
    shapes += [jax.ShapeDtypeStruct((192, down.shape[0]), f32 if k == 0 else bf16) for k in EMIT]
    return pl.pallas_call(
        hidden_kernel,
        in_specs=[pl.BlockSpec(memory_space=pltpu.SMEM)] + in_vmem(4),
        out_specs=in_vmem(len(shapes)),
        out_shape=shapes,
        compiler_params=pltpu.CompilerParams(**PARAMS),
        cost_estimate=pl.CostEstimate(flops=10**9, bytes_accessed=4 << 20, transcendentals=0),
        name="hidden",
    )(device, own, other, slots, down)


def table_grad_kernel(device, grads, early, late, far, out, kept, sems):
    core = device[0] & 1
    copies = []
    for j in range(4):
        half = core if j < 2 else 1 - core
        here = slice(j % 2 * CHUNK, (j % 2 + 1) * CHUNK)
        if j < 2:
            rows = jnp.concatenate([early[:, here], late[:, here]], axis=0)
        else:
            rows = far[:, here]
        kept[j] = jnp.dot(grads[...], rows, preferred_element_type=f32).astype(bf16)
        start = pl.multiple_of(half * SIDE + j % 2 * CHUNK, CHUNK)
        copies.append(
            pltpu.make_async_copy(kept.at[j], out.at[:, pl.ds(start, CHUNK)], sems.at[j])
        )
        copies[-1].start()
    for copy in copies:
        copy.wait()


def table_grad_call(device, grads, early, late, far):
    vocab, count = grads.shape
    return pl.pallas_call(
        table_grad_kernel,
        in_specs=[pl.BlockSpec(memory_space=pltpu.SMEM)] + in_vmem(4),
        out_specs=anywhere(1)[0],
        out_shape=jax.ShapeDtypeStruct((vocab, WIDTH), bf16),
        scratch_shapes=[pltpu.VMEM((4, vocab, CHUNK), bf16), pltpu.SemaphoreType.DMA((4,))],
        compiler_params=pltpu.CompilerParams(**PARAMS),
        cost_estimate=pl.CostEstimate(
            flops=2 * vocab * count * WIDTH, bytes_accessed=4 << 20, transcendentals=0
        ),
        name="table_grad",
    )(device, grads, early, late, far)


def local(states, positions, counts, targets, table, h_pre, w_down):
    dp, mp = lax.axis_index("dp"), lax.axis_index("mp")
    device = dp * 16 + mp
    where = device.astype(i32)[None]

    halves = prepare_call(where, positions, counts, targets, states)
    spread = jnp.broadcast_to(halves[None], (NZ, *halves.shape)).reshape(-1, *halves.shape[1:])
    zc_groups = [
        [spot(x, y, z, c) for z in range(NZ) for c in range(NC)]
        for x in range(NX)
        for y in range(NY)
    ]
    xy_groups = [
        [spot(x, y, z, c) for x in range(NX) for y in range(NY)]
        for z in range(NZ)
        for c in range(NC)
    ]
    block = lax.all_to_all(spread, BOTH, 0, 0, axis_index_groups=zc_groups, tiled=True)
    block = block.reshape(-1, SIDE + META)

    wide, tall = by_core(along_y, along_x), by_core(along_x, along_y)
    beside = {k: send(block, wide[k]) for k in (1, 3, 2)}
    block = jnp.concatenate([block] + [beside[k] for k in (1, 2, 3)], axis=0)
    low, high = block[: 2 * 48], block[2 * 48 :]
    one_low = send(low, tall[1])
    three_high = send(high, tall[3])
    one_high = send(high, tall[1])
    three_low = send(low, tall[3])
    two_low = send(one_low, tall[3])
    two_high = send(three_high, tall[1])
    spots = ((0, 0), (1, 0), (2, 2), (1, 2), (2, 0), (3, 0), (3, 2))
    pieces = [block, one_low, three_high, one_high, three_low]
    early = stacked(spots[:5], pieces, False, SIDE + META)
    (first_part,) = logits_call(where, table, early)
    first_part, two_low, two_high = lax.optimization_barrier((first_part, two_low, two_high))
    pieces += [two_low, two_high]
    crossing = [send(p, across) for p in pieces]
    late = stacked(((0, 0), (0, 2)), pieces[5:], False, SIDE + META)
    (last_part,) = logits_call(where, table, late)
    place, slot_of = ranks_call(where, early, late)
    far = stacked(spots, crossing, True, SIDE)
    logits, stats = logits_call(where, table, far, (first_part, last_part, place))

    def spread_merge(value, groups):
        count = len(groups[0])
        sent = jnp.broadcast_to(value[None], (count, *value.shape))
        got = lax.all_to_all(sent, BOTH, 0, 0, axis_index_groups=groups, tiled=True)
        return merged([got[:, 0], got[:, 1]])

    def merged(parts):
        tops, totals = parts
        largest = jnp.max(tops, axis=0)
        return jnp.stack([largest, jnp.sum(totals * jnp.exp(tops - largest), axis=0)])

    stats = spread_merge(stats, zc_groups)
    stats = spread_merge(stats, xy_groups)

    grads, keep, *away = dlogits_call(
        where, logits, place, stats, table
    )
    came = [send(a, across) for a in away]
    mine = own_call(where, keep, table)
    sums = [m + c.astype(f32) for m, c in zip(mine, came)]
    sums[0], h_pre = lax.optimization_barrier((sums[0], h_pre))
    activated, slope = gelu_call(where, h_pre)

    def scattered(chunks, along):
        return chunks[0], [send(chunks[k].astype(bf16), along[k]) for k in (1, 3, 2)]

    def total(own, parts):
        return sum([p.astype(f32) for p in parts], own)

    def relayed(own, one, three, two):
        half = own.shape[0] // 2
        low, high = slice(0, half), slice(half, None)
        via_one = send(two[low].astype(bf16), first[1])
        via_three = send(two[high].astype(bf16), first[3])
        plain_one = send(one[low].astype(bf16), first[1])
        plain_three = send(three[high].astype(bf16), first[3])
        joined_three = (three[low].astype(f32) + via_one.astype(f32)).astype(bf16)
        joined_one = (one[high].astype(f32) + via_three.astype(f32)).astype(bf16)
        joined_three = send(joined_three, first[3])
        joined_one = send(joined_one, first[1])
        return (
            total(own[low], [plain_one, joined_three]),
            total(own[high], [joined_one, plain_three]),
        )

    chunks = {k: sums[g] for g, k in enumerate(EMIT)}
    halves = relayed(chunks[0], chunks[1], chunks[3], chunks[2])
    *halves, activated, slope = lax.optimization_barrier((*halves, activated, slope))
    quarter = CHUNK // 4
    chunks = {
        j: jnp.concatenate([h[:, j * quarter : (j + 1) * quarter] for h in halves], axis=0)
        for j in range(4)
    }
    own, parts = scattered(chunks, second)
    width = total(own, parts)
    narrow = width.astype(bf16)
    width = total(width, [send(narrow, along_x[k]) for k in (1, 3, 2)])
    width = width + send(width, z_pair)
    width = width.astype(bf16)
    grad_rows, *chunks = hidden_call(where, width, send(width, across), slot_of, w_down)
    chunks = dict(zip(EMIT, chunks))
    block_rows = SLOTS // 16
    low, high = relayed(chunks[0], chunks[1], chunks[3], chunks[2])
    chunks = {j: (low, high)[j // 2][j % 2 * block_rows :][:block_rows] for j in range(4)}
    own, parts = scattered(chunks, second)
    hidden_grad = total(own, parts) * slope

    table_grad = table_grad_call(where, grads, early, late, far)
    w_down_grad = jnp.einsum("rf,rd->fd", activated, grad_rows, preferred_element_type=f32)
    return (table_grad, w_down_grad, hidden_grad)


def solution(mesh):
    in_specs = (
        P(BOTH, None),
        P(BOTH),
        P(BOTH),
        P(BOTH),
        P(BOTH, None),
        P(None, "mp"),
        P("mp", "dp"),
    )
    out_specs = (P(BOTH, None), P("mp", "dp"), P("dp", "mp"))
    return jax.shard_map(local, mesh=mesh, in_specs=in_specs, out_specs=out_specs, check_vma=False)
```

```python
import functools

import jax
import jax.numpy as jnp
import numpy as np
from jax import lax
from jax.experimental import pallas as pl
from jax.experimental.pallas import tpu as pltpu
from jax.sharding import PartitionSpec as P

half_root = 0.7071067811865476
density_scale = 0.3989422804014327
f32, bf16, i32 = jnp.float32, jnp.bfloat16, jnp.int32
NX, NY, NZ, NC = 4, 4, 8, 2
BOTH = ("dp", "mp")
SLOTS, LIVE, WIDTH, META, VOCAB_ROWS = 768, 384, 4096, 128, 496
HALF, CHUNK, SIDE = LIVE // 2, WIDTH // 4, WIDTH // 2
EMIT = (2, 1, 3, 0)
ORDER = (0, 1, 3, 2)
PARAMS = dict(vmem_limit_bytes=16 * 2**20)
EXACT = lax.Precision.HIGHEST


def spot(x, y, z, c):
    return (y * 4 + z // 2) * 16 + (z % 2) * 8 + x * 2 + c


PLACES = [(x, y, z, c) for x in range(NX) for y in range(NY) for z in range(NZ) for c in range(NC)]


def send(value, perm):
    return lax.ppermute(value, BOTH, perm)


def crossed(mx=0, my=0, mz=0, mc=0):
    return [(spot(x, y, z, c), spot(x ^ mx, y ^ my, z ^ mz, c ^ mc)) for x, y, z, c in PLACES]


across, z_pair = crossed(mc=1), crossed(mz=1)
along_x = {k: crossed(mx=k) for k in (1, 3, 2)}
along_y = {k: crossed(my=k) for k in (1, 3, 2)}
along_z = {k: crossed(mz=2 * k) for k in (1, 3, 2)}


def by_core(zero, one):
    return {k: [p for p in zero[k] if p[0] % 2 == 0] + [p for p in one[k] if p[0] % 2] for k in (1, 3, 2)}


first, second = by_core(along_y, along_z), by_core(along_z, along_y)


def dp_place(device, core, k, j):
    y_at, z_hi = device[0] >> 6, (device[0] >> 4) & 3
    return y_at ^ jnp.where(core == 0, k, j), z_hi ^ jnp.where(core == 0, j, k)


def rows_dot(a, b, **kw):
    return lax.dot_general(a, b, (((1,), (1,)), ((), ())), preferred_element_type=f32, **kw)


def gelu_slope(inputs):
    return (
        0.5 * (1.0 + lax.erf(inputs * half_root))
        + inputs * jnp.exp(-0.5 * inputs * inputs) * density_scale
    )


def digits(values):
    return [values % 256, (values // 256) % 256, values // 65536]


def one_hot(rank):
    return lax.broadcasted_iota(i32, (LIVE, rank.shape[1]), 0) == rank


def in_vmem(count):
    return [pl.BlockSpec(memory_space=pltpu.VMEM)] * count


def anywhere(count):
    return [pl.BlockSpec(memory_space=pl.ANY)] * count


def stack_kernel(spots, turned, *refs):
    *pieces, out = refs
    for (index, sub), piece in zip(spots, pieces):
        for row in range(0, piece.shape[0], 48):
            start = index * 192 + sub * 48 + row
            if turned:
                start = ORDER.index(sub + row // 48) * 192 + ORDER[index] * 48
            out[start : start + 48] = piece[row : row + 48, : out.shape[1]]


def stacked(spots, pieces, turned, columns):
    rows = sum(p.shape[0] for p in pieces)
    return pl.pallas_call(
        functools.partial(stack_kernel, spots, turned),
        in_specs=in_vmem(len(pieces)),
        out_specs=in_vmem(1)[0],
        out_shape=jax.ShapeDtypeStruct((rows, columns), bf16),
        compiler_params=pltpu.CompilerParams(**PARAMS),
        cost_estimate=pl.CostEstimate(flops=0, bytes_accessed=3 << 20, transcendentals=0),
        name="stacked",
    )(*pieces)


def prepare_kernel(device, *refs):
    sources, out, kept, sems = refs[:4], refs[4], refs[5:9], refs[9]
    copies = [pltpu.make_async_copy(s, k, sems.at[i]) for i, (s, k) in enumerate(zip(sources, kept))]
    for copy in copies:
        copy.start()
    for copy in copies:
        copy.wait()
    positions, counts, targets, states = kept
    cap = out.shape[1]
    row = lax.broadcasted_iota(i32, (8, META), 0)
    lane = lax.broadcasted_iota(i32, (8, META), 1)
    token, fields = jnp.full((8, META), -1, i32), jnp.zeros((8, META), i32)
    for s in range(cap):
        slot, target = device[0] * cap + s, targets[s]
        values = (
            slot & 255,
            slot >> 8,
            jnp.where(s < counts[0], 1, 0),
            target & 255,
            (target >> 8) & 255,
            target >> 16,
        )
        token = jnp.where(row == s, positions[s], token)
        for index, value in enumerate(values):
            fields = jnp.where((row == s) & (lane == index), value, fields)
    pick = (token == lane).astype(bf16)
    meta = fields.astype(f32).astype(bf16)
    rows = jnp.dot(pick, states[...], preferred_element_type=f32)
    for half in range(2):
        out[half, :, :SIDE] = rows[:cap, half * SIDE : (half + 1) * SIDE].astype(bf16)
        out[half, :, SIDE:] = meta[:cap]


def prepare_call(device, positions, counts, targets, states):
    shape = jax.ShapeDtypeStruct((2, positions.shape[0], SIDE + META), bf16)
    return pl.pallas_call(
        prepare_kernel,
        in_specs=[pl.BlockSpec(memory_space=pltpu.SMEM)] + anywhere(4),
        out_specs=in_vmem(1)[0],
        out_shape=shape,
        scratch_shapes=[pltpu.SMEM(a.shape, i32) for a in (positions, counts, targets)]
        + [pltpu.VMEM(states.shape, bf16), pltpu.SemaphoreType.DMA((4,))],
        compiler_params=pltpu.CompilerParams(vmem_limit_bytes=60 * 2**20),
        name="prepare",
    )(device, positions, counts, targets, states)


def ranks_kernel(device, early, late, place, slots):
    core = device[0] & 1
    meta = jnp.concatenate([early[...], late[...]], axis=0)
    pick = (
        lax.broadcasted_iota(i32, (8, META), 0) == lax.broadcasted_iota(i32, (8, META), 1)
    ).astype(bf16)
    rows = rows_dot(pick, meta)
    column = meta[:, :3].astype(f32)
    key, live = column[:, 0:1] + 256.0 * column[:, 1:2], column[:, 2:3]
    row_key, row_live = rows[0:1] + 256.0 * rows[1:2], rows[2:3]
    lane = lax.broadcasted_iota(i32, (1, LIVE), 1) + core * HALF
    own_rank = jnp.where(lane >= LIVE, lane - LIVE, lane).astype(f32)
    alive = row_live > 0.5
    rank = jnp.sum(jnp.where(key < row_key, live, 0.0), axis=0, keepdims=True)
    rank = jnp.where(alive, rank, -1.0).astype(i32)
    turn = rank + (1 - core) * HALF
    turn = jnp.where(turn >= LIVE, turn - LIVE, turn)
    turn = jnp.where(alive, turn, -1)
    label = [rows[k : k + 1].astype(i32) for k in (3, 4, 5)]
    label = label[0] + 256 * label[1] + 65536 * label[2] - device[0] * VOCAB_ROWS
    place[...] = jnp.concatenate([rank, turn, label] + [jnp.zeros_like(rank)] * 5, axis=0)
    down = jnp.sum(jnp.where(row_key < key, row_live, 0.0), axis=1, keepdims=True)
    hit = (down == own_rank) & (live > 0.5)
    slots[...] = jnp.sum(jnp.where(hit, key, 0.0), axis=0, keepdims=True).astype(i32)


def ranks_call(device, early, late):
    count = early.shape[0] + late.shape[0]
    whole = lambda shape: pl.BlockSpec(shape, lambda i: (0, 0))
    return pl.pallas_call(
        ranks_kernel,
        grid=(1,),
        in_specs=[
            pl.BlockSpec(memory_space=pltpu.SMEM),
            pl.BlockSpec((early.shape[0], META), lambda i: (0, SIDE // META)),
            pl.BlockSpec((late.shape[0], META), lambda i: (0, SIDE // META)),
        ],
        out_specs=[whole((8, count)), whole((1, LIVE))],
        out_shape=[jax.ShapeDtypeStruct((8, count), i32), jax.ShapeDtypeStruct((1, LIVE), i32)],
        compiler_params=pltpu.CompilerParams(**PARAMS),
        cost_estimate=pl.CostEstimate(flops=1 << 22, bytes_accessed=1 << 18, transcendentals=0),
        name="ranks",
    )(device, early, late)


def near_kernel(device, table, rows, logits):
    start = pl.multiple_of((device[0] & 1) * SIDE, SIDE)
    logits[...] = rows_dot(table[:, pl.ds(start, SIDE)], rows[:, :SIDE])


def far_kernel(device, table, rows, early, late, place, logits, stats):
    start = pl.multiple_of((1 - (device[0] & 1)) * SIDE, SIDE)
    partial = jnp.concatenate([early[...], late[...]], axis=1)
    values = partial + rows_dot(table[:, pl.ds(start, SIDE)], rows[:, :SIDE])
    logits[...] = values
    top = jnp.max(values, axis=0, keepdims=True)
    total = jnp.sum(jnp.exp(values - top), axis=0, keepdims=True)
    found = jnp.concatenate([top, total], axis=0)
    stats[...] = rows_dot(found, one_hot(place[0:1]).astype(f32), precision=EXACT)


def logits_call(device, table, rows, extra=()):
    vocab, count = table.shape[0], rows.shape[0]
    shapes = [jax.ShapeDtypeStruct((vocab, count), f32), jax.ShapeDtypeStruct((2, LIVE), f32)]
    shapes = shapes if extra else shapes[:1]
    return pl.pallas_call(
        far_kernel if extra else near_kernel,
        in_specs=[pl.BlockSpec(memory_space=pltpu.SMEM)] + in_vmem(2 + len(extra)),
        out_specs=in_vmem(len(shapes)),
        out_shape=shapes,
        compiler_params=pltpu.CompilerParams(**PARAMS),
        cost_estimate=pl.CostEstimate(
            flops=vocab * count * WIDTH, bytes_accessed=4 << 20, transcendentals=vocab * count
        ),
        name="logits",
    )(device, table, rows, *extra)


def chunk_dot(device, core, g, value, table):
    parts = []
    for j in range(4):
        y_to, z_to = dp_place(device, core, EMIT[g], j)
        start = pl.multiple_of(y_to * CHUNK + z_to * 256, 256)
        parts.append(jnp.dot(value, table[:, pl.ds(start, 256)], preferred_element_type=f32))
    return jnp.concatenate(parts, axis=1)


def dlogits_kernel(device, lg, place, stats, table, grads, keep, *outs):
    rank, turn, label = place[0:1], place[1:2], place[2:3]
    where = lax.dot_general(
        stats[...],
        one_hot(rank).astype(f32),
        (((1,), (0,)), ((), ())),
        preferred_element_type=f32,
        precision=EXACT,
    )
    alive = rank >= 0
    top = jnp.where(alive, where[0:1], 0.0)
    total = jnp.where(alive, where[1:2], 1.0)
    values = lg[...]
    soft = jnp.exp(values - top) / total
    hit = lax.broadcasted_iota(i32, values.shape, 0) == label
    grad = jnp.where(alive, soft - jnp.where(hit, 1.0, 0.0), 0.0).astype(bf16)
    grads[...] = grad
    packed = rows_dot(one_hot(turn).astype(bf16), grad).astype(bf16)
    keep[...] = packed[HALF:]
    theirs = packed[:HALF]
    for g, out in enumerate(outs):
        out[...] = chunk_dot(device, 1 - (device[0] & 1), g, theirs, table).astype(bf16)


def dlogits_call(device, logits, place, stats, table):
    vocab = table.shape[0]
    out_shapes = [jax.ShapeDtypeStruct((vocab, SLOTS), bf16)]
    out_shapes += [jax.ShapeDtypeStruct((HALF, vocab), bf16)]
    out_shapes += [jax.ShapeDtypeStruct((HALF, CHUNK), bf16)] * 4
    return pl.pallas_call(
        dlogits_kernel,
        in_specs=[pl.BlockSpec(memory_space=pltpu.SMEM)] + in_vmem(4),
        out_specs=in_vmem(6),
        out_shape=out_shapes,
        compiler_params=pltpu.CompilerParams(**PARAMS),
        cost_estimate=pl.CostEstimate(
            flops=2 * vocab * HALF * WIDTH, bytes_accessed=4 << 20, transcendentals=vocab * SLOTS
        ),
        name="dlogits",
    )(device, logits, place, stats, table)


def own_kernel(device, packed, table, *outs):
    for g, out in enumerate(outs):
        out[...] = chunk_dot(device, device[0] & 1, g, packed[...], table)


def own_call(device, packed, table):
    vocab = table.shape[0]
    return pl.pallas_call(
        own_kernel,
        in_specs=[pl.BlockSpec(memory_space=pltpu.SMEM)] + in_vmem(2),
        out_specs=in_vmem(4),
        out_shape=[jax.ShapeDtypeStruct((HALF, CHUNK), f32)] * 4,
        compiler_params=pltpu.CompilerParams(**PARAMS),
        cost_estimate=pl.CostEstimate(
            flops=2 * vocab * HALF * WIDTH, bytes_accessed=4 << 20, transcendentals=0
        ),
        name="own_width",
    )(device, packed, table)


def gelu_kernel(device, pre, active, slope):
    values = pre[...].astype(f32)
    active[...] = (0.5 * values * (1.0 + lax.erf(values * half_root))).astype(bf16)

    @pl.when(pl.program_id(0) == device[0] >> 6)
    def _():
        start = pl.multiple_of(((device[0] >> 4) & 3) * 48, 16)
        slope[...] = gelu_slope(pre[pl.ds(start, 48), :].astype(f32))


def gelu_call(device, pre):
    rows, units = pre.shape
    block = pl.BlockSpec((rows // 4, units), lambda i: (i, 0))
    return pl.pallas_call(
        gelu_kernel,
        grid=(4,),
        in_specs=[pl.BlockSpec(memory_space=pltpu.SMEM), block],
        out_specs=[block, pl.BlockSpec((48, units), lambda i: (0, 0))],
        out_shape=[
            jax.ShapeDtypeStruct((rows, units), bf16),
            jax.ShapeDtypeStruct((48, units), f32),
        ],
        compiler_params=pltpu.CompilerParams(**PARAMS),
        cost_estimate=pl.CostEstimate(
            flops=rows * units * 30, bytes_accessed=rows * units * 4, transcendentals=rows * units
        ),
        name="gelu",
    )(device, pre)


def hidden_chunks(device, rows, down, ks, outs):
    for k, out in zip(ks, outs):
        parts = []
        for j in range(4):
            y_to, z_to = dp_place(device, device[0] & 1, k, j)
            start = y_to * 192 + z_to * 48
            parts.append(rows[pl.ds(pl.multiple_of(start, 16), 48), :])
        out[...] = rows_dot(jnp.concatenate(parts, axis=0), down[...]).astype(out.dtype)


def lead_kernel(device, own, other, slots, down, rows, out):
    place = lax.broadcasted_iota(i32, (SLOTS, LIVE), 0) == slots[...]
    compact = jnp.concatenate([own[...], other[...]], axis=0)
    rows[...] = jnp.dot(place.astype(bf16), compact, preferred_element_type=f32).astype(bf16)
    hidden_chunks(device, rows, down, EMIT[:1], [out])


def rest_kernel(device, rows, down, *outs):
    hidden_chunks(device, rows, down, EMIT[1:], outs)


def hidden_call(device, own, other, slots, down):
    shapes = [
        jax.ShapeDtypeStruct((192, down.shape[0]), f32 if k == 0 else bf16) for k in EMIT
    ]

    def call(kernel, operands, outs, name):
        return pl.pallas_call(
            kernel,
            in_specs=[pl.BlockSpec(memory_space=pltpu.SMEM)] + in_vmem(len(operands)),
            out_specs=in_vmem(len(outs)),
            out_shape=outs,
            compiler_params=pltpu.CompilerParams(**PARAMS),
            cost_estimate=pl.CostEstimate(flops=5 * 10**8, bytes_accessed=2 << 20, transcendentals=0),
            name=name,
        )(device, *operands)

    whole = jax.ShapeDtypeStruct((SLOTS, own.shape[1]), bf16)
    rows, lead = call(lead_kernel, (own, other, slots, down), [whole] + shapes[:1], "hidden_lead")
    rest = call(rest_kernel, (rows, down), shapes[1:], "hidden_rest")
    return rows, lead, *rest


def table_grad_kernel(device, grads, early, late, far, out, kept, sems):
    core = device[0] & 1
    copies = []
    for j in range(4):
        half = core if j < 2 else 1 - core
        here = slice(j % 2 * CHUNK, (j % 2 + 1) * CHUNK)
        if j < 2:
            rows = jnp.concatenate([early[:, here], late[:, here]], axis=0)
        else:
            rows = far[:, here]
        kept[j] = jnp.dot(grads[...], rows, preferred_element_type=f32).astype(bf16)
        start = pl.multiple_of(half * SIDE + j % 2 * CHUNK, CHUNK)
        copies.append(
            pltpu.make_async_copy(kept.at[j], out.at[:, pl.ds(start, CHUNK)], sems.at[j])
        )
        copies[-1].start()
    for copy in copies:
        copy.wait()


def table_grad_call(device, grads, early, late, far):
    vocab, count = grads.shape
    return pl.pallas_call(
        table_grad_kernel,
        in_specs=[pl.BlockSpec(memory_space=pltpu.SMEM)] + in_vmem(4),
        out_specs=anywhere(1)[0],
        out_shape=jax.ShapeDtypeStruct((vocab, WIDTH), bf16),
        scratch_shapes=[pltpu.VMEM((4, vocab, CHUNK), bf16), pltpu.SemaphoreType.DMA((4,))],
        compiler_params=pltpu.CompilerParams(**PARAMS),
        cost_estimate=pl.CostEstimate(
            flops=2 * vocab * count * WIDTH, bytes_accessed=4 << 20, transcendentals=0
        ),
        name="table_grad",
    )(device, grads, early, late, far)


def local(states, positions, counts, targets, table, h_pre, w_down):
    dp, mp = lax.axis_index("dp"), lax.axis_index("mp")
    device = dp * 16 + mp
    where = device.astype(i32)[None]

    halves = prepare_call(where, positions, counts, targets, states)
    spread = jnp.broadcast_to(halves[None], (NZ, *halves.shape)).reshape(-1, *halves.shape[1:])
    zc_groups = [
        [spot(x, y, z, c) for z in range(NZ) for c in range(NC)]
        for x in range(NX)
        for y in range(NY)
    ]
    xy_groups = [
        [spot(x, y, z, c) for x in range(NX) for y in range(NY)]
        for z in range(NZ)
        for c in range(NC)
    ]
    block = lax.all_to_all(spread, BOTH, 0, 0, axis_index_groups=zc_groups, tiled=True)
    block = block.reshape(-1, SIDE + META)

    wide, tall = by_core(along_y, along_x), by_core(along_x, along_y)
    beside = {k: send(block, wide[k]) for k in (1, 3, 2)}
    block = jnp.concatenate([block] + [beside[k] for k in (1, 2, 3)], axis=0)
    low, high = block[: 2 * 48], block[2 * 48 :]
    one_low = send(low, tall[1])
    three_high = send(high, tall[3])
    one_high = send(high, tall[1])
    three_low = send(low, tall[3])
    two_low = send(one_low, tall[3])
    two_high = send(three_high, tall[1])
    spots = ((0, 0), (1, 0), (2, 2), (1, 2), (2, 0), (3, 0), (3, 2))
    pieces = [block, one_low, three_high, one_high, three_low]
    early = stacked(spots[:5], pieces, False, SIDE + META)
    (first_part,) = logits_call(where, table, early)
    first_part, two_low, two_high = lax.optimization_barrier((first_part, two_low, two_high))
    pieces += [two_low, two_high]
    crossing = [send(p, across) for p in pieces]
    late = stacked(((0, 0), (0, 2)), pieces[5:], False, SIDE + META)
    (last_part,) = logits_call(where, table, late)
    place, slot_of = ranks_call(where, early, late)
    far = stacked(spots, crossing, True, SIDE)
    logits, stats = logits_call(where, table, far, (first_part, last_part, place))

    def spread_merge(value, groups):
        count = len(groups[0])
        sent = jnp.broadcast_to(value[None], (count, *value.shape))
        got = lax.all_to_all(sent, BOTH, 0, 0, axis_index_groups=groups, tiled=True)
        return merged([got[:, 0], got[:, 1]])

    def merged(parts):
        tops, totals = parts
        largest = jnp.max(tops, axis=0)
        return jnp.stack([largest, jnp.sum(totals * jnp.exp(tops - largest), axis=0)])

    stats = spread_merge(stats, zc_groups)
    stats = spread_merge(stats, xy_groups)

    grads, keep, *away = dlogits_call(
        where, logits, place, stats, table
    )
    came = [send(a, across) for a in away]
    mine = own_call(where, keep, table)
    sums = [m + c.astype(f32) for m, c in zip(mine, came)]
    sums[0], h_pre = lax.optimization_barrier((sums[0], h_pre))
    activated, slope = gelu_call(where, h_pre)

    def scattered(chunks, along):
        return chunks[0], [send(chunks[k].astype(bf16), along[k]) for k in (1, 3, 2)]

    def total(own, parts):
        return sum([p.astype(f32) for p in parts], own)

    def relayed(own, one, three, two):
        half = own.shape[0] // 2
        low, high = slice(0, half), slice(half, None)
        via_one = send(two[low].astype(bf16), first[1])
        via_three = send(two[high].astype(bf16), first[3])
        plain_one = send(one[low].astype(bf16), first[1])
        plain_three = send(three[high].astype(bf16), first[3])
        joined_three = (three[low].astype(f32) + via_one.astype(f32)).astype(bf16)
        joined_one = (one[high].astype(f32) + via_three.astype(f32)).astype(bf16)
        joined_three = send(joined_three, first[3])
        joined_one = send(joined_one, first[1])
        return (
            total(own[low], [plain_one, joined_three]),
            total(own[high], [joined_one, plain_three]),
        )

    chunks = {k: sums[g] for g, k in enumerate(EMIT)}
    halves = relayed(chunks[0], chunks[1], chunks[3], chunks[2])
    *halves, activated, slope = lax.optimization_barrier((*halves, activated, slope))
    quarter = CHUNK // 4
    chunks = {
        j: jnp.concatenate([h[:, j * quarter : (j + 1) * quarter] for h in halves], axis=0)
        for j in range(4)
    }
    own, parts = scattered(chunks, second)
    width = total(own, parts)
    narrow = width.astype(bf16)
    width = total(width, [send(narrow, along_x[k]) for k in (1, 3, 2)])
    width = width + send(width, z_pair)
    width = width.astype(bf16)
    grad_rows, *chunks = hidden_call(where, width, send(width, across), slot_of, w_down)
    chunks = dict(zip(EMIT, chunks))
    block_rows = SLOTS // 16
    low, high = relayed(chunks[0], chunks[1], chunks[3], chunks[2])
    chunks = {j: (low, high)[j // 2][j % 2 * block_rows :][:block_rows] for j in range(4)}
    own, parts = scattered(chunks, second)
    hidden_grad = total(own, parts) * slope

    table_grad = table_grad_call(where, grads, early, late, far)
    w_down_grad = jnp.einsum("rf,rd->fd", activated, grad_rows, preferred_element_type=f32)
    return (table_grad, w_down_grad, hidden_grad)


def solution(mesh):
    in_specs = (
        P(BOTH, None),
        P(BOTH),
        P(BOTH),
        P(BOTH),
        P(BOTH, None),
        P(None, "mp"),
        P("mp", "dp"),
    )
    out_specs = (P(BOTH, None), P("mp", "dp"), P("dp", "mp"))
    return jax.shard_map(local, mesh=mesh, in_specs=in_specs, out_specs=out_specs, check_vma=False)
```
